256 devices in a mesh: gx: 32 (over z, x), gy: 8 (over y, core).
Axes of the slice: x: 4, y: 4, z: 8, core: 2. Of those that a mesh axis runs over, the one named last changes fastest.
Arguments:
- phase_label: int32 [512, 256, 128], P('gx', 'gy'), may hold values from 0 to 2
- tab_index: int32 [512, 256, 128], P('gx', 'gy'), may hold values from 0 to 63
- source_field: float32 [512, 256, 128], P('gx', 'gy'), may hold values from -8 to 8
- sigma_table: float32 [3], replicated, may hold values from 0.2 to 5
- pattern_gain: float32 [16, 64], replicated, may hold values from -6 to 6
Outputs:
- solution: float32 [16, 512, 256, 128], P(None, 'gx', 'gy')
- residual: float32 [16, 512, 256, 128], P(None, 'gx', 'gy')
The draws below stay inside these ranges and needn't reach their ends.
All inputs are finite; a program needn't handle non-finite values.
Results may differ from the reference program's by a relative error of at most 0.0003.
Values sent between devices are 32-bit elements; how exact they have to be, the bound alone decides.
A program may use at most 192 MiB of HBM per device.

```python
import math
import jax
import jax.numpy as jnp
import numpy as np
from jax import lax

S = 4
NRHS = 16
TABS = 64
PHASES = 3
NX = 512
NY = 256
NZ = 128


def draw_source_field(key, part):
    key = jax.random.fold_in(key, 7)
    first_key, second_key = jax.random.split(key, 2)
    across = jnp.arange(NX, dtype=jnp.float32) / max(NX - 1, 1)
    rising = (1.0 + 2.0 * across)[:, None, None]
    jitter = jax.random.uniform(second_key, (NX, NY, NZ), jnp.float32, 0.5, 2.0)
    normal_part = jax.random.normal(first_key, (NX, NY, NZ), jnp.float32)
    return jnp.clip(rising * jitter * normal_part, -8.0, 8.0)


def touch_ends(values, rng, least, high):
    shape = values.shape
    index_at = [jax.random.randint(jax.random.fold_in(rng, axis), (), 0, shape[axis]) for axis in range(len(shape))]
    values = values.at[tuple(index_at)].set(least)
    longest = shape.index(max(shape))
    index_at[longest] = (index_at[longest] + 1) % shape[longest]
    return values.at[tuple(index_at)].set(high)


def bell_draw(key, dims, spread, most, kind=jnp.bfloat16):
    return jnp.clip(spread * jax.random.normal(key, dims, jnp.float32), -most, most).astype(kind)


def setup_inputs(seed: int = 0) -> dict:
    keys = jax.random.split(jax.random.key(seed), 6)
    return {
        "phase_label": touch_ends(jax.random.randint(keys[0], (NX, NY, NZ), 0, PHASES), jax.random.fold_in(keys[0], 1), 0, PHASES - 1).astype(jnp.int32),
        "tab_index": touch_ends(jax.random.randint(keys[1], (NX, NY, NZ), 0, TABS), jax.random.fold_in(keys[1], 1), 0, TABS - 1).astype(jnp.int32),
        "source_field": draw_source_field(jax.random.fold_in(keys[5], 71), 0),
        "sigma_table": jnp.clip(jnp.exp(jax.random.uniform(keys[3], (PHASES,), jnp.float32, math.log(0.2), math.log(5.0))), 0.2, 5.0),
        "pattern_gain": bell_draw(keys[4], (NRHS, TABS), 1.0, 6.0, jnp.float32),
    }


OFFSETS = ((-1, 0, 0), (1, 0, 0), (0, -1, 0), (0, 1, 0), (0, 0, -1), (0, 0, 1))

def moved(array, a, b, c):
    sx = array.shape[-3]
    sy = array.shape[-2]
    sz = array.shape[-1]
    return array[..., 1 + a:sx - 1 + a, 1 + b:sy - 1 + b, 1 + c:sz - 1 + c]

def neighbour_mean(fields, conduct):
    fields_z = jnp.pad(fields, ((0, 0), (0, 0), (0, 0), (1, 1)))
    conduct_z = jnp.pad(conduct, ((0, 0), (0, 0), (1, 1)))
    centre = moved(conduct_z, 0, 0, 0)
    summed = jnp.zeros(fields.shape[:1] + centre.shape, jnp.float32)
    weights = jnp.zeros(centre.shape, jnp.float32)
    for offset in OFFSETS:
        face = 0.5 * (centre + moved(conduct_z, offset[0], offset[1], offset[2]))
        summed = summed + face[None] * moved(fields_z, offset[0], offset[1], offset[2])
        weights = weights + face
    inside = centre > 0
    return jnp.where(inside[None], summed / jnp.where(inside, weights, 1.0)[None], 0.0)

def difference_matrix():
    matrix = np.zeros((NRHS * (S + 1), NRHS * S), np.float32)
    for step in range(S):
        for column in range(NRHS):
            matrix[step * NRHS + column, step * NRHS + column] = 1.0
            matrix[(step + 1) * NRHS + column, step * NRHS + column] = -1.0
    return jnp.asarray(matrix)

def least_squares(gram):
    highest = lax.Precision.HIGHEST
    diff = difference_matrix()
    hess = jnp.dot(diff.T, jnp.dot(gram, diff, precision=highest), precision=highest)
    right_block = jnp.dot(diff.T, gram[:, :NRHS], precision=highest)
    factor = jnp.linalg.cholesky(hess)
    coeffs = jax.scipy.linalg.cho_solve((factor, True), right_block)
    return (diff, coeffs)

def finish(flat, shape):
    highest = lax.Precision.HIGHEST
    gram = jnp.dot(flat, flat.T, precision=highest)
    diff, coeffs = least_squares(gram)
    solution = jnp.dot(coeffs.T, flat[:S * NRHS], precision=highest)
    combined = jnp.dot(diff, coeffs, precision=highest)
    residual = flat[:NRHS] - jnp.dot(combined.T, flat, precision=highest)
    return (solution.reshape((NRHS,) + shape), residual.reshape((NRHS,) + shape))

def reference(phase_label, tab_index, source_field, sigma_table, pattern_gain):
    shape = phase_label.shape
    conduct = sigma_table[phase_label]
    start = pattern_gain[:, tab_index] * source_field[None]
    conduct_wide = jnp.pad(conduct, ((1, 1), (1, 1), (0, 0)))
    krylov = [start]
    current = start
    for step in range(S):
        padded = jnp.pad(current, ((0, 0), (1, 1), (1, 1), (0, 0)))
        current = neighbour_mean(padded, conduct_wide)
        krylov.append(current)
    flat = jnp.concatenate([field.reshape(NRHS, -1) for field in krylov], 0)
    return finish(flat, shape)
```

```python
import functools

import jax
import jax.numpy as jnp
from jax import lax
from jax.experimental import pallas as pl
from jax.experimental.pallas import tpu as pltpu
from jax.sharding import PartitionSpec as P

S = 4
NRHS = 16
LANES = 128
PAD = 8
CORES = 2
RING_X = 4
MESH = pl.DeviceIdType.MESH
F32 = jnp.float32
BF16 = jnp.bfloat16
ROWS = (S + 1) * NRHS
BASIS = S * NRHS


def split_hi_lo(value):
    high = value.astype(BF16)
    low = (value - high.astype(F32)).astype(BF16)
    return high, low


def krylov_kernel(nx, ny, phase_hbm, tab_hbm, source_hbm, sigma_ref, gain_ref, basis_hbm, total_ref,
                  phase_ext, tab_ext, source_ext, conduct, weight, f0, f1, f2, f3, basis, acc, packed,
                  part1, part2, part3, sum2, sum3,
                  own_sem, face_send, face_recv, basis_sem,
                  send1, recv1, send2, recv2, send3, recv3, send4, recv4):
    bx, by = phase_hbm.shape[0], phase_hbm.shape[1]
    ex = bx + 2 * S
    ey = by + 2 * S
    gx, gy = lax.axis_index("gx"), lax.axis_index("gy")
    xi, zi = lax.rem(gx, RING_X), lax.div(gx, RING_X)
    yi, ci = lax.div(gy, CORES), lax.rem(gy, CORES)
    ring_y = ny // CORES
    ring_z = nx // RING_X
    right, left = lax.rem(gx + 1, nx), lax.rem(gx + nx - 1, nx)
    up, down = lax.rem(gy + 1, ny), lax.rem(gy + ny - 1, ny)

    def at_y(o):
        return gx, lax.rem(gy + o, ny)

    def at_x(o):
        return zi * RING_X + lax.rem(xi + o, RING_X), gy

    def at_z(o):
        return lax.rem(zi + o, ring_z) * RING_X + xi, gy

    def at_row(o):
        return gx, lax.rem(yi + o, ring_y) * CORES + ci

    faces = ((right, gy), (left, gy), (right, up), (right, down), (left, up), (left, down))
    peers = faces + tuple(at_y(o) for o in range(1, ny)) + tuple(at_x(o) for o in range(1, RING_X)) + tuple(
        at_z(o) for o in range(1, ring_z))
    barrier = pltpu.get_barrier_semaphore()
    for peer in peers:
        pl.semaphore_signal(barrier, inc=1, device_id=peer, device_id_type=MESH)

    inputs = (phase_hbm, tab_hbm, source_hbm)
    wide = (phase_ext, tab_ext, source_ext)
    own_copies = []
    for a in range(3):
        copy = pltpu.make_async_copy(inputs[a], wide[a].at[pl.ds(S, bx), pl.ds(PAD, by)], own_sem.at[a])
        copy.start()
        own_copies.append(copy)
    for a in range(3):
        corner = jnp.zeros((PAD, LANES), wide[a].dtype)
        for x in (0, ex - 1):
            for y in (0, PAD + by):
                wide[a][x, y : y + PAD, :] = corner
    pl.semaphore_wait(barrier, len(peers))

    x_all, y_all = (0, bx), (0, by)
    x_top, x_low = (bx - S, S), (0, S)
    x_top3, x_low3 = (bx - S + 1, S - 1), (0, S - 1)
    y_top, y_low = (by - PAD, PAD), (0, PAD)
    routes = (
        ((gx, up), x_all, y_top, S, 0),
        ((gx, down), x_all, y_low, S, PAD + by),
        ((right, gy), x_top, y_all, 0, PAD),
        ((left, gy), x_low, y_all, S + bx, PAD),
        ((right, up), x_top3, y_top, 1, 0),
        ((right, down), x_top3, y_low, 1, PAD + by),
        ((left, up), x_low3, y_top, S + bx, 0),
        ((left, down), x_low3, y_low, S + bx, PAD + by),
    )
    face_copies = []
    for r, (peer, xs, ys, dx, dy) in enumerate(routes):
        for a in range(3):
            copy = pltpu.make_async_remote_copy(
                src_ref=inputs[a].at[pl.ds(*xs), pl.ds(*ys)],
                dst_ref=wide[a].at[pl.ds(dx, xs[1]), pl.ds(dy, ys[1])],
                send_sem=face_send.at[r, a],
                recv_sem=face_recv.at[r, a],
                device_id=peer,
                device_id_type=MESH,
            )
            copy.start()
            face_copies.append(copy)

    sigma0, sigma1, sigma2 = sigma_ref[0], sigma_ref[1], sigma_ref[2]
    gain = gain_ref[...]
    lane = lax.broadcasted_iota(jnp.int32, (PAD * 2 + by, LANES), 1)
    row_y = lax.broadcasted_iota(jnp.int32, (PAD * 2 + by, LANES), 0) + (gy * by - PAD)
    in_y = (row_y >= 0) & (row_y < ny * by)

    def start_columns(x, columns):
        for j in columns:
            tab = jnp.broadcast_to(tab_ext[x, pl.ds(j + PAD - S, 1), :], (NRHS, LANES))
            source = jnp.broadcast_to(source_ext[x, pl.ds(j + PAD - S, 1), :], (NRHS, LANES))
            picked = jnp.take_along_axis(gain, tab, axis=1, mode="promise_in_bounds")
            f0[x, j] = picked * source

    def mask_row(x):
        row_x = gx * bx + x - S
        inside = in_y & (row_x >= 0) & (row_x < nx * bx)
        phase = phase_ext[x]
        value = jnp.where(phase == 0, sigma0, jnp.where(phase == 1, sigma1, sigma2))
        conduct[x] = jnp.where(inside, value, 0.0)
        source_ext[x] = jnp.where(inside, source_ext[x], 0.0)

    def weight_row(x):
        c = conduct[x]
        zero = jnp.zeros_like(c)
        rows = by + 2 * PAD
        xm = c + conduct[x - 1]
        xp = c + conduct[x + 1]
        ym = c + pltpu.roll(c, 1, 0)
        yp = c + pltpu.roll(c, rows - 1, 0)
        low, top = lane > 0, lane < LANES - 1
        zm = c + jnp.where(low, pltpu.roll(c, 1, 1), zero)
        zp = c + jnp.where(top, pltpu.roll(c, LANES - 1, 1), zero)
        total = ((xm + xp) + (ym + yp)) + (zm + zp)
        inside = c > 0
        inverse = jnp.where(inside, 1.0 / jnp.where(inside, total, 1.0), 0.0)
        weight[0, x] = xm * inverse
        weight[1, x] = xp * inverse
        weight[2, x] = ym * inverse
        weight[3, x] = yp * inverse
        weight[4, x] = jnp.where(low, zm * inverse, zero)
        weight[5, x] = jnp.where(top, zp * inverse, zero)

    def mean_row(src, x, m, store):
        before, centre = src[x, m - 1], src[x, m]
        for j in range(m, ey - m):
            after = src[x, j + 1]
            w = [jnp.broadcast_to(weight[d, x, pl.ds(j + PAD - S, 1), :], (NRHS, LANES)) for d in range(6)]
            value = (w[0] * src[x - 1, j] + w[1] * src[x + 1, j]) + (w[2] * before + w[3] * after)
            value = value + (w[4] * pltpu.roll(centre, 1, 1) + w[5] * pltpu.roll(centre, LANES - 1, 1))
            store(j, value)
            before, centre = centre, after

    fields = (f0, f1, f2, f3)

    def inner_row(m):
        def body(x, carry):
            def store(j, value):
                fields[m][x, j] = value

            mean_row(fields[m - 1], x, m, store)
            return carry

        return body

    def last_row(x, carry):
        row = x - S

        def store(j, value):
            column = j - S
            values = [fields[m][x, j] for m in range(S)] + [value]
            for m in range(S + 1):
                high, low = split_hi_lo(values[m])
                basis[row, column, pl.ds(m * NRHS, NRHS), :] = high
                basis[row, column, pl.ds(ROWS + m * NRHS, NRHS), :] = low

        mean_row(fields[S - 1], x, S, store)
        pltpu.make_async_copy(basis.at[row], basis_hbm.at[row], basis_sem.at[row]).start()
        step = 8
        for first in range(0, by, step):
            block = jnp.concatenate([basis[row, first + k] for k in range(step)], axis=1)
            acc[...] += lax.dot_general(
                block[:ROWS], block, (((1,), (1,)), ((), ())), preferred_element_type=F32
            )
        return carry

    def rows_of(first, count, body):
        lax.fori_loop(first, first + count, body, 0)

    def two_sides(m, body):
        def both(r, carry):
            x = jnp.where(r < S, m + r, bx + S - m + r)
            return body(x, carry)

        return both

    for copy in own_copies:
        copy.wait()

    acc[...] = jnp.zeros_like(acc)

    def start_own(x, carry):
        start_columns(x, range(S, S + by))
        return carry

    rows_of(S, bx, start_own)
    for copy in face_copies[:6]:
        copy.wait_recv()

    def mask_own(x, carry):
        mask_row(x)
        start_columns(x, tuple(range(S)) + tuple(range(S + by, ey)))
        return carry

    def weight_own(x, carry):
        weight_row(x)
        return carry

    rows_of(S, bx, mask_own)
    rows_of(S + 1, bx - 2, weight_own)
    for m in range(1, S):
        rows_of(S + m, bx - 2 * m, inner_row(m))
    rows_of(2 * S, bx - 2 * S, last_row)

    for copy in face_copies[6:]:
        copy.wait_recv()

    def mask_far(x, carry):
        mask_row(x)
        start_columns(x, range(ey))
        return carry

    rows_of(0, S, mask_far)
    rows_of(S + bx, S, mask_far)
    rows_of(1, S, weight_own)
    rows_of(S + bx - 1, S, weight_own)
    for m in range(1, S):
        rows_of(m, S, inner_row(m))
        rows_of(S + bx - m, S, inner_row(m))
    rows_of(S, S, last_row)
    rows_of(bx, S, last_row)

    both = acc[...]
    lane_g = lax.broadcasted_iota(jnp.int32, (ROWS, LANES), 1)
    first = both[:, :LANES]
    second = jnp.concatenate([both[:, LANES:], jnp.zeros((ROWS, 2 * LANES - 2 * ROWS), F32)], axis=1)
    cross = pltpu.roll(jnp.where(lane_g >= ROWS, first, second), LANES - ROWS, 1)
    cross = jnp.where(lane_g < ROWS, cross, 0.0)
    square = jnp.concatenate([cross, jnp.zeros((LANES - ROWS, LANES), F32)], axis=0)
    gram = first + cross + square.T[:ROWS]
    lane_b = lane_g[:NRHS]
    blocks = [gram[m * NRHS : (m + 1) * NRHS] for m in range(S + 1)]
    top = jnp.where(lane_b < ROWS, blocks[0], pltpu.roll(blocks[2], 48, 1))
    low = jnp.where(
        lane_b < ROWS,
        blocks[1],
        jnp.where(lane_b < 112, pltpu.roll(blocks[3], 32, 1), pltpu.roll(blocks[4], 48, 1)),
    )
    packed[0] = top[:8]
    packed[1] = top[8:]
    packed[2] = low[:8]
    packed[3] = low[8:]

    def exchange(peers_of, source_of, slots, slot, send, recv):
        copies = []
        for k, peer in enumerate(peers_of):
            copy = pltpu.make_async_remote_copy(
                src_ref=source_of(peer),
                dst_ref=slots.at[slot],
                send_sem=send.at[k],
                recv_sem=recv.at[k],
                device_id=peer,
                device_id_type=MESH,
            )
            copy.start()
            copies.append(copy)
        for copy in copies:
            copy.wait()

    part1[gy] = packed[yi]
    exchange([at_y(o) for o in range(1, ny)], lambda peer: packed.at[lax.div(peer[1], CORES)], part1, gy, send1, recv1)
    sum2[...] = jnp.sum(part1[...], axis=0)
    part2[xi] = sum2[...]
    exchange([at_x(o) for o in range(1, RING_X)], lambda peer: sum2, part2, xi, send2, recv2)
    sum3[...] = jnp.sum(part2[...], axis=0)
    part3[zi] = sum3[...]
    exchange([at_z(o) for o in range(1, ring_z)], lambda peer: sum3, part3, zi, send3, recv3)
    total_ref[yi] = jnp.sum(part3[...], axis=0)
    exchange([at_row(o) for o in range(1, ring_y)], lambda peer: total_ref.at[yi], total_ref, yi, send4, recv4)

    for copy in face_copies:
        copy.wait_send()
    for row in range(bx):
        pltpu.make_async_copy(basis.at[row], basis_hbm.at[row], basis_sem.at[row]).wait()


def combine_kernel(basis_hbm, total_ref, sol_hbm, res_hbm, basis, sol, res, left_ref, basis_sem, sol_sem, res_sem):
    bx, by = basis_hbm.shape[0], basis_hbm.shape[1]

    def load(x):
        return pltpu.make_async_copy(basis_hbm.at[x], basis.at[x], basis_sem.at[x])

    for x in range(bx):
        load(x).start()

    top = jnp.concatenate([total_ref[0], total_ref[1]], axis=0)
    low = jnp.concatenate([total_ref[2], total_ref[3]], axis=0)
    blocks = [top, low, pltpu.roll(top, 80, 1), pltpu.roll(low, 96, 1), pltpu.roll(low, 80, 1)]
    upper = jnp.concatenate(blocks + [jnp.zeros((LANES - ROWS, LANES), F32)], axis=0)
    lane = lax.broadcasted_iota(jnp.int32, (LANES, LANES), 1)
    row = lax.broadcasted_iota(jnp.int32, (LANES, LANES), 0)
    keep = (lane // NRHS >= row // NRHS) & (lane < ROWS)
    upper = jnp.where(keep, upper, 0.0)
    gram = jnp.where(keep, upper, upper.T)
    down = gram[:BASIS] - gram[NRHS : BASIS + NRHS]
    lane64, row64 = lane[:BASIS], row[:BASIS]
    hess = down - pltpu.roll(down, LANES - NRHS, 1)
    work = jnp.where(lane64 < BASIS, hess, jnp.where(lane64 < ROWS, pltpu.roll(down, BASIS, 1), 0.0))
    for j in range(BASIS):
        pivot = work[j : j + 1, :]
        scaled = pivot / pivot[:, j : j + 1]
        column = work[:, j : j + 1]
        work = jnp.where(row64 == j, scaled, work - column * scaled)
    coeffs = jnp.where(lane64 < NRHS, pltpu.roll(work, LANES - BASIS, 1), 0.0)
    gap = jnp.zeros((NRHS, LANES), F32)
    full = jnp.concatenate([coeffs, gap], axis=0)
    moved = jnp.concatenate([gap, coeffs], axis=0)
    unit = jnp.where(lane[:ROWS] == row[:ROWS], 1.0, 0.0)
    unit = jnp.where(lane[:ROWS] < NRHS, unit, 0.0)
    other = unit - (full - moved)
    pair = full + pltpu.roll(other, NRHS, 1)
    tall = jnp.concatenate([pair, pair, jnp.zeros((2 * LANES - 2 * ROWS, LANES), F32)], axis=0)
    table = jnp.concatenate([tall[:LANES].T, tall[LANES:].T], axis=1)[: 2 * NRHS]
    high, low_part = split_hi_lo(table)
    left_ref[...] = jnp.concatenate([high, low_part], axis=0)
    left = left_ref[:, : 2 * ROWS]

    def body(x, carry):
        load(x).wait()
        for y in range(0, by, 2):
            right = jnp.concatenate([basis[x, y], basis[x, y + 1]], axis=1)
            both = jnp.dot(left, right, preferred_element_type=F32)
            both = both[: 2 * NRHS] + both[2 * NRHS :]
            for k in range(2):
                part = both[:, k * LANES : (k + 1) * LANES]
                sol[x, pl.ds(y + k, NRHS, stride=by), :] = part[:NRHS]
                res[x, pl.ds(y + k, NRHS, stride=by), :] = part[NRHS:]
        for p in range(NRHS):
            pltpu.make_async_copy(sol.at[x, pl.ds(p * by, by)], sol_hbm.at[p, x], sol_sem.at[x, p]).start()
            pltpu.make_async_copy(res.at[x, pl.ds(p * by, by)], res_hbm.at[p, x], res_sem.at[x, p]).start()
        return carry

    lax.fori_loop(0, bx, body, 0)

    def drain(x, carry):
        for p in range(NRHS):
            pltpu.make_async_copy(sol.at[x, pl.ds(p * by, by)], sol_hbm.at[p, x], sol_sem.at[x, p]).wait()
            pltpu.make_async_copy(res.at[x, pl.ds(p * by, by)], res_hbm.at[p, x], res_sem.at[x, p]).wait()
        return carry

    lax.fori_loop(0, bx, drain, 0)


def krylov_call(nx, ny, phase_label, tab_index, source_field, sigma_table, gain):
    bx, by = phase_label.shape[0], phase_label.shape[1]
    ex, ey = bx + 2 * S, by + 2 * S
    wide = (ex, by + 2 * PAD, LANES)
    ring_y, ring_z = ny // CORES, nx // RING_X
    hbm = pl.BlockSpec(memory_space=pl.ANY)
    vmem = pl.BlockSpec(memory_space=pltpu.VMEM)
    dma = pltpu.SemaphoreType.DMA
    tile = (8, LANES)
    return pl.pallas_call(
        functools.partial(krylov_kernel, nx, ny),
        out_shape=(
            jax.ShapeDtypeStruct((bx, by, 2 * ROWS, LANES), BF16),
            jax.ShapeDtypeStruct((ring_y,) + tile, F32),
        ),
        in_specs=[hbm, hbm, hbm, pl.BlockSpec(memory_space=pltpu.SMEM), vmem],
        out_specs=(hbm, vmem),
        scratch_shapes=[
            pltpu.VMEM(wide, jnp.int32),
            pltpu.VMEM(wide, jnp.int32),
            pltpu.VMEM(wide, F32),
            pltpu.VMEM(wide, F32),
            pltpu.VMEM((6,) + wide, F32),
        ]
        + [pltpu.VMEM((ex, ey, NRHS, LANES), F32)] * S
        + [
            pltpu.VMEM((bx, by, 2 * ROWS, LANES), BF16),
            pltpu.VMEM((ROWS, 2 * ROWS), F32),
            pltpu.VMEM((ring_y,) + tile, F32),
            pltpu.VMEM((ny,) + tile, F32),
            pltpu.VMEM((RING_X,) + tile, F32),
            pltpu.VMEM((ring_z,) + tile, F32),
            pltpu.VMEM(tile, F32),
            pltpu.VMEM(tile, F32),
            dma((3,)),
            dma((8, 3)),
            dma((8, 3)),
            dma((bx,)),
            dma((ny - 1,)),
            dma((ny - 1,)),
            dma((RING_X - 1,)),
            dma((RING_X - 1,)),
            dma((ring_z - 1,)),
            dma((ring_z - 1,)),
            dma((ring_y - 1,)),
            dma((ring_y - 1,)),
        ],
        compiler_params=pltpu.CompilerParams(
            collective_id=0, has_side_effects=True, vmem_limit_bytes=62 * 2**20
        ),
    )(phase_label, tab_index, source_field, sigma_table, gain)


def combine_call(basis, total):
    bx, by = basis.shape[0], basis.shape[1]
    hbm = pl.BlockSpec(memory_space=pl.ANY)
    vmem = pl.BlockSpec(memory_space=pltpu.VMEM)
    dma = pltpu.SemaphoreType.DMA
    out = jax.ShapeDtypeStruct((NRHS, bx, by, LANES), F32)
    return pl.pallas_call(
        combine_kernel,
        out_shape=(out, out),
        in_specs=[hbm, vmem],
        out_specs=(hbm, hbm),
        scratch_shapes=[
            pltpu.VMEM(basis.shape, BF16),
            pltpu.VMEM((bx, NRHS * by, LANES), F32),
            pltpu.VMEM((bx, NRHS * by, LANES), F32),
            pltpu.VMEM((4 * NRHS, 2 * LANES), BF16),
            dma((bx,)),
            dma((bx, NRHS)),
            dma((bx, NRHS)),
        ],
        compiler_params=pltpu.CompilerParams(vmem_limit_bytes=56 * 2**20),
    )(basis, total)


def solution(mesh):
    nx, ny = mesh.shape["gx"], mesh.shape["gy"]

    def shards(phase_label, tab_index, source_field, sigma_table, pattern_gain):
        gain = jnp.pad(pattern_gain, ((0, 0), (0, LANES - pattern_gain.shape[1])))
        basis, total = krylov_call(nx, ny, phase_label, tab_index, source_field, sigma_table, gain)
        return combine_call(basis, total)

    return jax.shard_map(
        shards,
        mesh=mesh,
        in_specs=(P("gx", "gy", None), P("gx", "gy", None), P("gx", "gy", None), P(), P()),
        out_specs=(P(None, "gx", "gy", None), P(None, "gx", "gy", None)),
        check_vma=False,
    )
```

```python
import functools

import jax
import jax.numpy as jnp
from jax import lax
from jax.experimental import pallas as pl
from jax.experimental.pallas import tpu as pltpu
from jax.sharding import PartitionSpec as P

S = 4
NRHS = 16
LANES = 128
PAD = 8
RING_X = 4
MESH = pl.DeviceIdType.MESH
F32 = jnp.float32
BF16 = jnp.bfloat16
ROWS = (S + 1) * NRHS
BASIS = S * NRHS


def split_hi_lo(value):
    high = value.astype(BF16)
    low = (value - high.astype(F32)).astype(BF16)
    return high, low


def lane_pick(table, index):
    numbers = lax.GatherDimensionNumbers(
        offset_dims=(),
        collapsed_slice_dims=(1,),
        start_index_map=(1,),
        operand_batching_dims=(0,),
        start_indices_batching_dims=(0,),
    )
    return lax.gather(
        table, index[..., None], numbers, (1, 1), mode=lax.GatherScatterMode.PROMISE_IN_BOUNDS
    )


def krylov_kernel(nx, ny, phase_hbm, tab_hbm, source_hbm, sigma_ref, gain_ref, basis_hbm, total_ref,
                  phase_own, tab_ext, wide, conduct, charge, weight, f0, f1, f2, f3, f4, acc,
                  part1, part2, part3, own_sem, face_send, face_recv, basis_sem, ring_send, ring_recv):
    bx, by = phase_hbm.shape[0], phase_hbm.shape[1]
    ex = bx + 2 * S
    ey = by + 2 * S
    gx, gy = lax.axis_index("gx"), lax.axis_index("gy")
    xi, zi = lax.rem(gx, RING_X), lax.div(gx, RING_X)
    ring_z = nx // RING_X
    right, left = lax.rem(gx + 1, nx), lax.rem(gx + nx - 1, nx)
    up, down = lax.rem(gy + 1, ny), lax.rem(gy + ny - 1, ny)

    def at_y(o):
        return gx, lax.rem(gy + o, ny)

    def at_x(o):
        return zi * RING_X + lax.rem(xi + o, RING_X), gy

    def at_z(o):
        return lax.rem(zi + o, ring_z) * RING_X + xi, gy

    faces = ((right, gy), (left, gy), (right, up), (right, down), (left, up), (left, down))
    peers = faces + tuple(at_y(o) for o in range(1, ny)) + tuple(at_x(o) for o in range(1, RING_X)) + tuple(
        at_z(o) for o in range(1, ring_z))
    barrier = pltpu.get_barrier_semaphore()
    for peer in peers:
        pl.semaphore_signal(barrier, inc=1, device_id=peer, device_id_type=MESH)

    own = (pl.ds(S, bx), pl.ds(PAD, by))
    own_copies = [
        pltpu.make_async_copy(phase_hbm, phase_own, own_sem.at[0]),
        pltpu.make_async_copy(tab_hbm, tab_ext.at[own], own_sem.at[1]),
        pltpu.make_async_copy(source_hbm, wide.at[(2,) + own], own_sem.at[2]),
    ]
    for copy in own_copies:
        copy.start()
    corner = jnp.zeros((PAD, LANES), F32)
    for a in range(3):
        for x in (0, ex - 1):
            for y in (0, PAD + by):
                wide[a, x, y : y + PAD, :] = corner
    acc[...] = jnp.zeros_like(acc)
    sigma0, sigma1, sigma2 = sigma_ref[0], sigma_ref[1], sigma_ref[2]
    gain = jnp.concatenate([gain_ref[...], jnp.zeros((NRHS, LANES - gain_ref.shape[1]), F32)], axis=1)
    for copy in own_copies:
        copy.wait()

    def fill_row(r, carry):
        phase = phase_own[r]
        value = jnp.where(phase == 0, sigma0, jnp.where(phase == 1, sigma1, sigma2))
        wide[0, r + S, PAD : PAD + by, :] = value
        wide[1, r + S, PAD : PAD + by, :] = tab_ext[r + S, PAD : PAD + by, :].astype(F32)
        return carry

    lax.fori_loop(0, bx, fill_row, 0, unroll=4)
    pl.semaphore_wait(barrier, len(peers))

    x_all, y_all = (0, bx), (0, by)
    x_top, x_low = (bx - S, S), (0, S)
    x_top3, x_low3 = (bx - S + 1, S - 1), (0, S - 1)
    y_top, y_low = (by - PAD, PAD), (0, PAD)
    routes = (
        ((right, gy), x_top, y_all, 0, PAD),
        ((left, gy), x_low, y_all, S + bx, PAD),
        ((gx, up), x_all, y_top, S, 0),
        ((gx, down), x_all, y_low, S, PAD + by),
        ((right, up), x_top3, y_top, 1, 0),
        ((right, down), x_top3, y_low, 1, PAD + by),
        ((left, up), x_low3, y_top, S + bx, 0),
        ((left, down), x_low3, y_low, S + bx, PAD + by),
    )
    face_copies = []
    for r, (peer, xs, ys, dx, dy) in enumerate(routes):
        copy = pltpu.make_async_remote_copy(
            src_ref=wide.at[:, pl.ds(S + xs[0], xs[1]), pl.ds(PAD + ys[0], ys[1])],
            dst_ref=wide.at[:, pl.ds(dx, xs[1]), pl.ds(dy, ys[1])],
            send_sem=face_send.at[r],
            recv_sem=face_recv.at[r],
            device_id=peer,
            device_id_type=MESH,
        )
        copy.start()
        face_copies.append(copy)

    lane = lax.broadcasted_iota(jnp.int32, (PAD * 2 + by, LANES), 1)
    row_y = lax.broadcasted_iota(jnp.int32, (PAD * 2 + by, LANES), 0) + (gy * by - PAD)
    in_y = (row_y >= 0) & (row_y < ny * by)

    def start_columns(x, columns, strength):
        for j in columns:
            tab = jnp.broadcast_to(tab_ext[x, pl.ds(j + PAD - S, 1), :], (NRHS, LANES))
            f0[x, j] = lane_pick(gain, tab) * jnp.broadcast_to(strength(j + PAD - S), (NRHS, LANES))

    def start_own(x, carry):
        start_columns(x, range(S, S + by), lambda y: wide[2, x, pl.ds(y, 1), :])
        return carry

    def mask_row(x, sides):
        row_x = gx * bx + x - S
        inside = in_y & (row_x >= 0) & (row_x < nx * bx)
        conduct[x] = jnp.where(inside, wide[0, x], 0.0)
        charge[x] = jnp.where(inside, wide[2, x], 0.0)
        for first, count in sides:
            tab_ext[x, first : first + count, :] = wide[1, x, first : first + count, :].astype(jnp.int32)

    def mask_own(x, carry):
        mask_row(x, ((0, PAD), (PAD + by, PAD)))
        start_columns(x, tuple(range(S)) + tuple(range(S + by, ey)), lambda y: charge[x, pl.ds(y, 1), :])
        return carry

    def mask_far(x, carry):
        mask_row(x, ((0, 2 * PAD + by),))
        start_columns(x, range(ey), lambda y: charge[x, pl.ds(y, 1), :])
        return carry

    def weight_row(x, carry):
        c = conduct[x]
        zero = jnp.zeros_like(c)
        rows = by + 2 * PAD
        xm = c + conduct[x - 1]
        xp = c + conduct[x + 1]
        ym = c + pltpu.roll(c, 1, 0)
        yp = c + pltpu.roll(c, rows - 1, 0)
        low, top = lane > 0, lane < LANES - 1
        zm = c + jnp.where(low, pltpu.roll(c, 1, 1), zero)
        zp = c + jnp.where(top, pltpu.roll(c, LANES - 1, 1), zero)
        total = ((xm + xp) + (ym + yp)) + (zm + zp)
        inside = c > 0
        inverse = jnp.where(inside, 1.0 / jnp.where(inside, total, 1.0), 0.0)
        weight[0, x] = xm * inverse
        weight[1, x] = xp * inverse
        weight[2, x] = ym * inverse
        weight[3, x] = yp * inverse
        weight[4, x] = jnp.where(low, zm * inverse, zero)
        weight[5, x] = jnp.where(top, zp * inverse, zero)
        return carry

    def mean_rows(src, x, count, m, columns, before, centre, store):
        for j in columns:
            after = [src[x + r, j + 1] for r in range(count)]
            edge = [src[x - 1, j]] + centre + [src[x + count, j]]
            for r in range(count):
                w = [jnp.broadcast_to(weight[d, x + r, pl.ds(j + PAD - S, 1), :], (NRHS, LANES)) for d in range(6)]
                value = (w[0] * edge[r] + w[1] * edge[r + 2]) + (w[2] * before[r] + w[3] * after[r])
                value = value + (w[4] * pltpu.roll(centre[r], 1, 1) + w[5] * pltpu.roll(centre[r], LANES - 1, 1))
                store(r, j, value)
            before, centre = centre, after
        return before, centre

    fields = (f0, f1, f2, f3)

    def inner_rows(m, first):
        def body(i, carry):
            x = first + 2 * i

            def store(r, j, value):
                fields[m][x + r, j] = value

            src = fields[m - 1]
            before = [src[x + r, m - 1] for r in range(2)]
            centre = [src[x + r, m] for r in range(2)]
            mean_rows(src, x, 2, m, range(m, ey - m), before, centre, store)
            return carry

        return body

    def last_row(x, carry):
        row = x - S
        step = 8
        before, centre = [f3[x, S - 1]], [f3[x, S]]
        for first in range(S, S + by, step):
            newest = {}

            def store(r, j, value):
                newest[j] = value
                f4[row, j - S] = value

            before, centre = mean_rows(f3, x, 1, S, range(first, first + step), before, centre, store)
            columns = []
            for j in range(first, first + step):
                parts = [split_hi_lo(value) for value in [field[x, j] for field in fields] + [newest[j]]]
                columns.append(jnp.concatenate([p[0] for p in parts] + [p[1] for p in parts], axis=0))
            block = jnp.concatenate(columns, axis=1)
            acc[...] += lax.dot_general(
                block, block[:ROWS], (((1,), (1,)), ((), ())), preferred_element_type=F32
            )
        return carry

    def rows_of(first, count, body):
        lax.fori_loop(first, first + count, body, 0)

    def pairs_of(m, first, count):
        lax.fori_loop(0, count // 2, inner_rows(m, first), 0)

    def keep(m, first, count):
        src = f4.at[pl.ds(first, count)] if m == S else fields[m].at[pl.ds(S + first, count), pl.ds(S, by)]
        pltpu.make_async_copy(src, basis_hbm.at[m, pl.ds(first, count)], basis_sem).start()

    rows_of(S, bx, start_own)
    keep(0, 0, bx)
    for copy in face_copies[2:4]:
        copy.wait_recv()
    rows_of(S, bx, mask_own)
    rows_of(S + 1, bx - 2, weight_row)
    for m in range(1, S):
        pairs_of(m, S + m, bx - 2 * m)
        keep(m, m, bx - 2 * m)
    rows_of(2 * S, bx - 2 * S, last_row)
    keep(S, S, bx - 2 * S)

    for copy in face_copies[:2] + face_copies[4:]:
        copy.wait_recv()
    rows_of(0, S, mask_far)
    rows_of(S + bx, S, mask_far)
    rows_of(1, S, weight_row)
    rows_of(S + bx - 1, S, weight_row)
    for m in range(1, S):
        pairs_of(m, m, S)
        pairs_of(m, S + bx - m, S)
        keep(m, 0, m)
        keep(m, bx - m, m)
    rows_of(S, S, last_row)
    rows_of(bx, S, last_row)
    keep(S, 0, S)
    keep(S, bx - S, S)

    both = acc[...]
    both = both[:ROWS] + both[ROWS:]
    gram = jnp.concatenate([both, jnp.zeros((ROWS, LANES - ROWS), F32)], axis=1)
    lane_b = lax.broadcasted_iota(jnp.int32, (NRHS, LANES), 1)
    blocks = [gram[m * NRHS : (m + 1) * NRHS] for m in range(S + 1)]
    part1[gy, :NRHS] = blocks[0] + jnp.where(lane_b < ROWS, 0.0, pltpu.roll(blocks[2], 48, 1))
    part1[gy, NRHS:] = jnp.where(
        lane_b < ROWS,
        blocks[1],
        jnp.where(lane_b < 112, pltpu.roll(blocks[3], 32, 1), pltpu.roll(blocks[4], 48, 1)),
    )

    sends = []

    def spread(k, peers_of, slots, slot):
        copies = []
        for peer in peers_of:
            copy = pltpu.make_async_remote_copy(
                src_ref=slots.at[slot],
                dst_ref=slots.at[slot],
                send_sem=ring_send.at[k],
                recv_sem=ring_recv.at[k],
                device_id=peer,
                device_id_type=MESH,
            )
            copy.start()
            copies.append(copy)
        others = slots.at[pl.ds(0, len(copies))]
        whole = pltpu.make_async_copy(others, others, ring_recv.at[k])
        whole.wait()
        sends.append(pltpu.make_async_copy(others, others, ring_send.at[k]))
        return jnp.sum(slots[...], axis=0)

    part2[xi] = spread(0, [at_y(o) for o in range(1, ny)], part1, gy)
    part3[zi] = spread(1, [at_x(o) for o in range(1, RING_X)], part2, xi)
    total_ref[...] = spread(2, [at_z(o) for o in range(1, ring_z)], part3, zi)

    for send in sends:
        send.wait()
    for copy in face_copies:
        copy.wait_send()
    pltpu.make_async_copy(basis_hbm, basis_hbm, basis_sem).wait()


def solve_table(total):
    top, low = total[:NRHS], total[NRHS:]
    blocks = [top, low, pltpu.roll(top, 80, 1), pltpu.roll(low, 96, 1), pltpu.roll(low, 80, 1)]
    upper = jnp.concatenate(blocks + [jnp.zeros((LANES - ROWS, LANES), F32)], axis=0)
    lane = lax.broadcasted_iota(jnp.int32, (LANES, LANES), 1)
    row = lax.broadcasted_iota(jnp.int32, (LANES, LANES), 0)
    keep = (lane // NRHS >= row // NRHS) & (lane < ROWS)
    upper = jnp.where(keep, upper, 0.0)
    gram = jnp.where(keep, upper, upper.T)
    down = gram[:BASIS] - gram[NRHS : BASIS + NRHS]
    lane64, row64 = lane[:BASIS], row[:BASIS]
    hess = down - pltpu.roll(down, LANES - NRHS, 1)
    work = jnp.where(lane64 < BASIS, hess, jnp.where(lane64 < ROWS, pltpu.roll(down, BASIS, 1), 0.0))
    for j in range(BASIS):
        pivot = work[j : j + 1, :]
        scaled = pivot / pivot[:, j : j + 1]
        column = work[:, j : j + 1]
        work = jnp.where(row64 == j, scaled, work - column * scaled)
    coeffs = jnp.where(lane64 < NRHS, pltpu.roll(work, LANES - BASIS, 1), 0.0)
    gap = jnp.zeros((NRHS, LANES), F32)
    full = jnp.concatenate([coeffs, gap], axis=0)
    moved = jnp.concatenate([gap, coeffs], axis=0)
    unit = jnp.where((lane[:ROWS] == row[:ROWS]) & (lane[:ROWS] < NRHS), 1.0, 0.0)
    pair = full + pltpu.roll(unit - (full - moved), NRHS, 1)
    tall = jnp.concatenate([pair, pair, jnp.zeros((2 * LANES - 2 * ROWS, LANES), F32)], axis=0)
    return jnp.concatenate([tall[:LANES].T, tall[LANES:].T], axis=1)[: 2 * NRHS]


def combine_kernel(basis_hbm, total_ref, sol_hbm, res_hbm, basis, sol, res, left_ref, basis_sem, sol_sem, res_sem):
    bx, by = basis_hbm.shape[1], basis_hbm.shape[2]
    group = bx // basis_sem.shape[0]

    def load(g):
        rows = pl.ds(g * group, group)
        return pltpu.make_async_copy(basis_hbm.at[:, rows], basis.at[:, rows], basis_sem.at[g])

    for g in range(bx // group):
        load(g).start()

    high, low = split_hi_lo(solve_table(total_ref[...]))
    left_ref[...] = jnp.concatenate([high, low], axis=0)
    left = left_ref[:, : 2 * ROWS]

    def combine_row(x):
        for y in range(0, by, 2):
            columns = []
            for k in range(2):
                parts = [split_hi_lo(basis[m, x, y + k]) for m in range(S + 1)]
                columns.append(jnp.concatenate([p[0] for p in parts] + [p[1] for p in parts], axis=0))
            both = jnp.dot(left, jnp.concatenate(columns, axis=1), preferred_element_type=F32)
            both = both[: 2 * NRHS] + both[2 * NRHS :]
            for k in range(2):
                part = both[:, k * LANES : (k + 1) * LANES]
                sol.at[x].reshape(NRHS * by, LANES)[pl.ds(y + k, NRHS, stride=by), :] = part[:NRHS]
                res.at[x].reshape(NRHS * by, LANES)[pl.ds(y + k, NRHS, stride=by), :] = part[NRHS:]
        pltpu.make_async_copy(sol.at[x], sol_hbm.at[:, x], sol_sem).start()
        pltpu.make_async_copy(res.at[x], res_hbm.at[:, x], res_sem).start()

    def body(g, carry):
        load(g).wait()
        for r in range(group):
            combine_row(g * group + r)
        return carry

    lax.fori_loop(0, bx // group, body, 0)
    pltpu.make_async_copy(sol_hbm, sol_hbm, sol_sem).wait()
    pltpu.make_async_copy(res_hbm, res_hbm, res_sem).wait()


def krylov_call(nx, ny, phase_label, tab_index, source_field, sigma_table, gain):
    bx, by = phase_label.shape[0], phase_label.shape[1]
    ex, ey = bx + 2 * S, by + 2 * S
    wide = (ex, by + 2 * PAD, LANES)
    ring_z = nx // RING_X
    hbm = pl.BlockSpec(memory_space=pl.ANY)
    vmem = pl.BlockSpec(memory_space=pltpu.VMEM)
    dma = pltpu.SemaphoreType.DMA
    packed = (2 * NRHS, LANES)
    return pl.pallas_call(
        functools.partial(krylov_kernel, nx, ny),
        out_shape=(
            jax.ShapeDtypeStruct((S + 1, bx, by, NRHS, LANES), F32),
            jax.ShapeDtypeStruct(packed, F32),
        ),
        in_specs=[hbm, hbm, hbm, pl.BlockSpec(memory_space=pltpu.SMEM), vmem],
        out_specs=(hbm, vmem),
        scratch_shapes=[
            pltpu.VMEM((bx, by, LANES), jnp.int32),
            pltpu.VMEM(wide, jnp.int32),
            pltpu.VMEM((3,) + wide, F32),
            pltpu.VMEM(wide, F32),
            pltpu.VMEM(wide, F32),
            pltpu.VMEM((6,) + wide, F32),
        ]
        + [pltpu.VMEM((ex, ey, NRHS, LANES), F32)] * S
        + [
            pltpu.VMEM((bx, by, NRHS, LANES), F32),
            pltpu.VMEM((2 * ROWS, ROWS), F32),
            pltpu.VMEM((ny,) + packed, F32),
            pltpu.VMEM((RING_X,) + packed, F32),
            pltpu.VMEM((ring_z,) + packed, F32),
            dma((3,)),
            dma((8,)),
            dma((8,)),
            dma(()),
            dma((3,)),
            dma((3,)),
        ],
        compiler_params=pltpu.CompilerParams(
            collective_id=0, has_side_effects=True, vmem_limit_bytes=56 * 2**20
        ),
    )(phase_label, tab_index, source_field, sigma_table, gain)


def combine_call(basis, total):
    bx, by = basis.shape[1], basis.shape[2]
    hbm = pl.BlockSpec(memory_space=pl.ANY)
    vmem = pl.BlockSpec(memory_space=pltpu.VMEM)
    dma = pltpu.SemaphoreType.DMA
    out = jax.ShapeDtypeStruct((NRHS, bx, by, LANES), F32)
    return pl.pallas_call(
        combine_kernel,
        out_shape=(out, out),
        in_specs=[hbm, vmem],
        out_specs=(hbm, hbm),
        scratch_shapes=[
            pltpu.VMEM(basis.shape, F32),
            pltpu.VMEM((bx, NRHS, by, LANES), F32),
            pltpu.VMEM((bx, NRHS, by, LANES), F32),
            pltpu.VMEM((4 * NRHS, 2 * LANES), BF16),
            dma((bx // 2,)),
            dma(()),
            dma(()),
        ],
        compiler_params=pltpu.CompilerParams(vmem_limit_bytes=56 * 2**20),
    )(basis, total)


def solution(mesh):
    nx, ny = mesh.shape["gx"], mesh.shape["gy"]

    def shards(phase_label, tab_index, source_field, sigma_table, pattern_gain):
        basis, total = krylov_call(nx, ny, phase_label, tab_index, source_field, sigma_table, pattern_gain)
        return combine_call(basis, total)

    return jax.shard_map(
        shards,
        mesh=mesh,
        in_specs=(P("gx", "gy", None), P("gx", "gy", None), P("gx", "gy", None), P(), P()),
        out_specs=(P(None, "gx", "gy", None), P(None, "gx", "gy", None)),
        check_vma=False,
    )
```

```python
import functools

import jax
import jax.numpy as jnp
from jax import lax
from jax.experimental import pallas as pl
from jax.experimental.pallas import tpu as pltpu
from jax.sharding import PartitionSpec as P

S = 4
NRHS = 16
LANES = 128
PAD = 8
RING_X = 4
MESH = pl.DeviceIdType.MESH
F32 = jnp.float32
BF16 = jnp.bfloat16
ROWS = (S + 1) * NRHS
BASIS = S * NRHS


def split_hi_lo(value):
    high = value.astype(BF16)
    low = (value - high.astype(F32)).astype(BF16)
    return high, low


def lane_pick(table, index):
    numbers = lax.GatherDimensionNumbers(
        offset_dims=(),
        collapsed_slice_dims=(1,),
        start_index_map=(1,),
        operand_batching_dims=(0,),
        start_indices_batching_dims=(0,),
    )
    return lax.gather(
        table, index[..., None], numbers, (1, 1), mode=lax.GatherScatterMode.PROMISE_IN_BOUNDS
    )


def krylov_kernel(nx, ny, phase_hbm, tab_hbm, source_hbm, sigma_ref, gain_ref, basis_hbm, total_ref,
                  phase_own, tab_ext, wide, conduct, charge, weight, f0, f1, f2, f3, f4, acc,
                  part1, part2, part3, own_sem, face_send, face_recv, basis_sem, ring_send, ring_recv):
    bx, by = phase_hbm.shape[0], phase_hbm.shape[1]
    ex = bx + 2 * S
    ey = by + 2 * S
    gx, gy = lax.axis_index("gx"), lax.axis_index("gy")
    xi, zi = lax.rem(gx, RING_X), lax.div(gx, RING_X)
    ring_z = nx // RING_X
    right, left = lax.rem(gx + 1, nx), lax.rem(gx + nx - 1, nx)
    up, down = lax.rem(gy + 1, ny), lax.rem(gy + ny - 1, ny)

    def at_y(o):
        return gx, lax.rem(gy + o, ny)

    def at_x(o):
        return zi * RING_X + lax.rem(xi + o, RING_X), gy

    def at_z(o):
        return lax.rem(zi + o, ring_z) * RING_X + xi, gy

    faces = ((right, gy), (left, gy), (right, up), (right, down), (left, up), (left, down))
    peers = faces + tuple(at_y(o) for o in range(1, ny)) + tuple(at_x(o) for o in range(1, RING_X)) + tuple(
        at_z(o) for o in range(1, ring_z))
    barrier = pltpu.get_barrier_semaphore()
    for peer in peers:
        pl.semaphore_signal(barrier, inc=1, device_id=peer, device_id_type=MESH)

    own = (pl.ds(S, bx), pl.ds(PAD, by))
    own_copies = [
        pltpu.make_async_copy(phase_hbm, phase_own, own_sem.at[0]),
        pltpu.make_async_copy(tab_hbm, tab_ext.at[own], own_sem.at[1]),
        pltpu.make_async_copy(source_hbm, wide.at[(2,) + own], own_sem.at[2]),
    ]
    for copy in own_copies:
        copy.start()
    corner = jnp.zeros((PAD, LANES), F32)
    for a in range(3):
        for x in (0, ex - 1):
            for y in (0, PAD + by):
                wide[a, x, y : y + PAD, :] = corner
    acc[...] = jnp.zeros_like(acc)
    sigma0, sigma1, sigma2 = sigma_ref[0], sigma_ref[1], sigma_ref[2]
    gain = jnp.concatenate([gain_ref[...], jnp.zeros((NRHS, LANES - gain_ref.shape[1]), F32)], axis=1)
    for copy in own_copies:
        copy.wait()

    def fill_row(r, carry):
        phase = phase_own[r]
        value = jnp.where(phase == 0, sigma0, jnp.where(phase == 1, sigma1, sigma2))
        wide[0, r + S, PAD : PAD + by, :] = value
        wide[1, r + S, PAD : PAD + by, :] = tab_ext[r + S, PAD : PAD + by, :].astype(F32)
        return carry

    lax.fori_loop(0, bx, fill_row, 0, unroll=4)
    pl.semaphore_wait(barrier, len(peers))

    x_all, y_all = (0, bx), (0, by)
    x_top, x_low = (bx - S, S), (0, S)
    x_top3, x_low3 = (bx - S + 1, S - 1), (0, S - 1)
    y_top, y_low = (by - PAD, PAD), (0, PAD)
    routes = (
        ((right, gy), x_top, y_all, 0, PAD),
        ((left, gy), x_low, y_all, S + bx, PAD),
        ((gx, up), x_all, y_top, S, 0),
        ((gx, down), x_all, y_low, S, PAD + by),
        ((right, up), x_top3, y_top, 1, 0),
        ((right, down), x_top3, y_low, 1, PAD + by),
        ((left, up), x_low3, y_top, S + bx, 0),
        ((left, down), x_low3, y_low, S + bx, PAD + by),
    )
    face_copies = []
    for r, (peer, xs, ys, dx, dy) in enumerate(routes):
        copy = pltpu.make_async_remote_copy(
            src_ref=wide.at[:, pl.ds(S + xs[0], xs[1]), pl.ds(PAD + ys[0], ys[1])],
            dst_ref=wide.at[:, pl.ds(dx, xs[1]), pl.ds(dy, ys[1])],
            send_sem=face_send.at[r],
            recv_sem=face_recv.at[r],
            device_id=peer,
            device_id_type=MESH,
        )
        copy.start()
        face_copies.append(copy)

    lane = lax.broadcasted_iota(jnp.int32, (PAD * 2 + by, LANES), 1)
    row_y = lax.broadcasted_iota(jnp.int32, (PAD * 2 + by, LANES), 0) + (gy * by - PAD)
    in_y = (row_y >= 0) & (row_y < ny * by)

    def start_columns(x, columns, strength):
        for j in columns:
            tab = jnp.broadcast_to(tab_ext[x, pl.ds(j + PAD - S, 1), :], (NRHS, LANES))
            f0[x, j] = lane_pick(gain, tab) * jnp.broadcast_to(strength(j + PAD - S), (NRHS, LANES))

    def start_own(x, carry):
        start_columns(x, range(S, S + by), lambda y: wide[2, x, pl.ds(y, 1), :])
        return carry

    def mask_row(x, sides):
        row_x = gx * bx + x - S
        inside = in_y & (row_x >= 0) & (row_x < nx * bx)
        conduct[x] = jnp.where(inside, wide[0, x], 0.0)
        charge[x] = jnp.where(inside, wide[2, x], 0.0)
        for first, count in sides:
            tab_ext[x, first : first + count, :] = wide[1, x, first : first + count, :].astype(jnp.int32)

    def mask_own(x, carry):
        mask_row(x, ((0, PAD), (PAD + by, PAD)))
        start_columns(x, tuple(range(S)) + tuple(range(S + by, ey)), lambda y: charge[x, pl.ds(y, 1), :])
        return carry

    def mask_far(x, carry):
        mask_row(x, ((0, 2 * PAD + by),))
        start_columns(x, range(ey), lambda y: charge[x, pl.ds(y, 1), :])
        return carry

    def weight_row(x, carry):
        c = conduct[x]
        zero = jnp.zeros_like(c)
        rows = by + 2 * PAD
        xm = c + conduct[x - 1]
        xp = c + conduct[x + 1]
        ym = c + pltpu.roll(c, 1, 0)
        yp = c + pltpu.roll(c, rows - 1, 0)
        low, top = lane > 0, lane < LANES - 1
        zm = c + jnp.where(low, pltpu.roll(c, 1, 1), zero)
        zp = c + jnp.where(top, pltpu.roll(c, LANES - 1, 1), zero)
        total = ((xm + xp) + (ym + yp)) + (zm + zp)
        inside = c > 0
        inverse = jnp.where(inside, 1.0 / jnp.where(inside, total, 1.0), 0.0)
        weight[0, x] = xm * inverse
        weight[1, x] = xp * inverse
        weight[2, x] = ym * inverse
        weight[3, x] = yp * inverse
        weight[4, x] = jnp.where(low, zm * inverse, zero)
        weight[5, x] = jnp.where(top, zp * inverse, zero)
        return carry

    def mean_rows(src, x, count, m, columns, before, centre, store):
        for j in columns:
            after = [src[x + r, j + 1] for r in range(count)]
            edge = [src[x - 1, j]] + centre + [src[x + count, j]]
            for r in range(count):
                w = [jnp.broadcast_to(weight[d, x + r, pl.ds(j + PAD - S, 1), :], (NRHS, LANES)) for d in range(6)]
                value = (w[0] * edge[r] + w[1] * edge[r + 2]) + (w[2] * before[r] + w[3] * after[r])
                value = value + (w[4] * pltpu.roll(centre[r], 1, 1) + w[5] * pltpu.roll(centre[r], LANES - 1, 1))
                store(r, j, value)
            before, centre = centre, after
        return before, centre

    fields = (f0, f1, f2, f3)

    def inner_rows(m, first):
        def body(i, carry):
            x = first + 2 * i

            def store(r, j, value):
                fields[m][x + r, j] = value

            src = fields[m - 1]
            before = [src[x + r, m - 1] for r in range(2)]
            centre = [src[x + r, m] for r in range(2)]
            mean_rows(src, x, 2, m, range(m, ey - m), before, centre, store)
            return carry

        return body

    def last_row(x, carry):
        row = x - S
        step = 8
        before, centre = [f3[x, S - 1]], [f3[x, S]]
        for first in range(S, S + by, step):
            newest = {}

            def store(r, j, value):
                newest[j] = value
                f4[row, j - S] = value

            before, centre = mean_rows(f3, x, 1, S, range(first, first + step), before, centre, store)
            columns = []
            for j in range(first, first + step):
                parts = [split_hi_lo(value) for value in [field[x, j] for field in fields] + [newest[j]]]
                columns.append(jnp.concatenate([p[0] for p in parts] + [p[1] for p in parts], axis=0))
            block = jnp.concatenate(columns, axis=1)
            acc[...] += lax.dot_general(
                block[:ROWS], block, (((1,), (1,)), ((), ())), preferred_element_type=F32
            )
        return carry

    def rows_of(first, count, body):
        lax.fori_loop(first, first + count, body, 0)

    def pairs_of(m, first, count):
        lax.fori_loop(0, count // 2, inner_rows(m, first), 0)

    def keep(m, first, count):
        src = f4.at[pl.ds(first, count)] if m == S else fields[m].at[pl.ds(S + first, count), pl.ds(S, by)]
        pltpu.make_async_copy(src, basis_hbm.at[m, pl.ds(first, count)], basis_sem).start()

    rows_of(S, bx, start_own)
    keep(0, 0, bx)
    for copy in face_copies[2:4]:
        copy.wait_recv()
    rows_of(S, bx, mask_own)
    rows_of(S + 1, bx - 2, weight_row)
    for m in range(1, S):
        pairs_of(m, S + m, bx - 2 * m)
        keep(m, m, bx - 2 * m)
    rows_of(2 * S, bx - 2 * S, last_row)
    keep(S, S, bx - 2 * S)

    for copy in face_copies[:2] + face_copies[4:]:
        copy.wait_recv()
    rows_of(0, S, mask_far)
    rows_of(S + bx, S, mask_far)
    rows_of(1, S, weight_row)
    rows_of(S + bx - 1, S, weight_row)
    for m in range(1, S):
        pairs_of(m, m, S)
        pairs_of(m, S + bx - m, S)
        keep(m, 0, m)
        keep(m, bx - m, m)
    rows_of(S, S, last_row)
    rows_of(bx, S, last_row)
    keep(S, 0, S)
    keep(S, bx - S, S)

    both = acc[...]
    lane_g = lax.broadcasted_iota(jnp.int32, (ROWS, LANES), 1)
    first = both[:, :LANES]
    second = jnp.concatenate([both[:, LANES:], jnp.zeros((ROWS, 2 * LANES - 2 * ROWS), F32)], axis=1)
    cross = pltpu.roll(jnp.where(lane_g >= ROWS, first, second), LANES - ROWS, 1)
    cross = jnp.where(lane_g < ROWS, cross, 0.0)
    square = jnp.concatenate([cross, jnp.zeros((LANES - ROWS, LANES), F32)], axis=0)
    gram = jnp.where(lane_g < ROWS, first, 0.0) + cross + square.T[:ROWS]
    lane_b = lane_g[:NRHS]
    blocks = [gram[m * NRHS : (m + 1) * NRHS] for m in range(S + 1)]
    part1[gy, :NRHS] = blocks[0] + jnp.where(lane_b < ROWS, 0.0, pltpu.roll(blocks[2], 48, 1))
    part1[gy, NRHS:] = jnp.where(
        lane_b < ROWS,
        blocks[1],
        jnp.where(lane_b < 112, pltpu.roll(blocks[3], 32, 1), pltpu.roll(blocks[4], 48, 1)),
    )

    sends = []

    def spread(k, peers_of, slots, slot):
        copies = []
        for peer in peers_of:
            copy = pltpu.make_async_remote_copy(
                src_ref=slots.at[slot],
                dst_ref=slots.at[slot],
                send_sem=ring_send.at[k],
                recv_sem=ring_recv.at[k],
                device_id=peer,
                device_id_type=MESH,
            )
            copy.start()
            copies.append(copy)
        others = slots.at[pl.ds(0, len(copies))]
        whole = pltpu.make_async_copy(others, others, ring_recv.at[k])
        whole.wait()
        sends.append(pltpu.make_async_copy(others, others, ring_send.at[k]))
        return jnp.sum(slots[...], axis=0)

    part2[xi] = spread(0, [at_y(o) for o in range(1, ny)], part1, gy)
    part3[zi] = spread(1, [at_x(o) for o in range(1, RING_X)], part2, xi)
    total_ref[...] = spread(2, [at_z(o) for o in range(1, ring_z)], part3, zi)

    for send in sends:
        send.wait()
    for copy in face_copies:
        copy.wait_send()
    pltpu.make_async_copy(basis_hbm, basis_hbm, basis_sem).wait()


def solve_table(total):
    top, low = total[:NRHS], total[NRHS:]
    blocks = [top, low, pltpu.roll(top, 80, 1), pltpu.roll(low, 96, 1), pltpu.roll(low, 80, 1)]
    upper = jnp.concatenate(blocks + [jnp.zeros((LANES - ROWS, LANES), F32)], axis=0)
    lane = lax.broadcasted_iota(jnp.int32, (LANES, LANES), 1)
    row = lax.broadcasted_iota(jnp.int32, (LANES, LANES), 0)
    keep = (lane // NRHS >= row // NRHS) & (lane < ROWS)
    upper = jnp.where(keep, upper, 0.0)
    gram = jnp.where(keep, upper, upper.T)
    down = gram[:BASIS] - gram[NRHS : BASIS + NRHS]
    lane64, row64 = lane[:BASIS], row[:BASIS]
    hess = down - pltpu.roll(down, LANES - NRHS, 1)
    work = jnp.where(lane64 < BASIS, hess, jnp.where(lane64 < ROWS, pltpu.roll(down, BASIS, 1), 0.0))
    for j in range(BASIS):
        pivot = work[j : j + 1, :]
        scaled = pivot / pivot[:, j : j + 1]
        column = work[:, j : j + 1]
        work = jnp.where(row64 == j, scaled, work - column * scaled)
    coeffs = jnp.where(lane64 < NRHS, pltpu.roll(work, LANES - BASIS, 1), 0.0)
    gap = jnp.zeros((NRHS, LANES), F32)
    full = jnp.concatenate([coeffs, gap], axis=0)
    moved = jnp.concatenate([gap, coeffs], axis=0)
    unit = jnp.where((lane[:ROWS] == row[:ROWS]) & (lane[:ROWS] < NRHS), 1.0, 0.0)
    pair = full + pltpu.roll(unit - (full - moved), NRHS, 1)
    tall = jnp.concatenate([pair, pair, jnp.zeros((2 * LANES - 2 * ROWS, LANES), F32)], axis=0)
    return jnp.concatenate([tall[:LANES].T, tall[LANES:].T], axis=1)[: 2 * NRHS]


def combine_kernel(basis_hbm, total_ref, sol_hbm, res_hbm, basis, sol, res, left_ref, basis_sem, sol_sem, res_sem):
    bx, by = basis_hbm.shape[1], basis_hbm.shape[2]
    group = bx // basis_sem.shape[0]
    pitch = sol.shape[2]

    def load(g):
        rows = pl.ds(g * group, group)
        return pltpu.make_async_copy(basis_hbm.at[:, rows], basis.at[:, rows], basis_sem.at[g])

    for g in range(bx // group):
        load(g).start()

    high, low = split_hi_lo(solve_table(total_ref[...]))
    left_ref[...] = jnp.concatenate([high, low], axis=0)
    left = left_ref[:, : 2 * ROWS]

    def combine_row(x):
        for y in range(0, by, 2):
            columns = []
            for k in range(2):
                parts = [split_hi_lo(basis[m, x, y + k]) for m in range(S + 1)]
                columns.append(jnp.concatenate([p[0] for p in parts] + [p[1] for p in parts], axis=0))
            both = jnp.dot(left, jnp.concatenate(columns, axis=1), preferred_element_type=F32)
            both = both[: 2 * NRHS] + both[2 * NRHS :]
            for k in range(2):
                part = both[:, k * LANES : (k + 1) * LANES]
                sol.at[x].reshape(NRHS * pitch, LANES)[pl.ds(y + k, NRHS, stride=pitch), :] = part[:NRHS]
                res.at[x].reshape(NRHS * pitch, LANES)[pl.ds(y + k, NRHS, stride=pitch), :] = part[NRHS:]
        pltpu.make_async_copy(sol.at[x, :, pl.ds(0, by)], sol_hbm.at[:, x], sol_sem).start()
        pltpu.make_async_copy(res.at[x, :, pl.ds(0, by)], res_hbm.at[:, x], res_sem).start()

    def body(g, carry):
        load(g).wait()
        for r in range(group):
            combine_row(g * group + r)
        return carry

    lax.fori_loop(0, bx // group, body, 0)
    pltpu.make_async_copy(sol_hbm, sol_hbm, sol_sem).wait()
    pltpu.make_async_copy(res_hbm, res_hbm, res_sem).wait()


def krylov_call(nx, ny, phase_label, tab_index, source_field, sigma_table, gain):
    bx, by = phase_label.shape[0], phase_label.shape[1]
    ex, ey = bx + 2 * S, by + 2 * S
    wide = (ex, by + 2 * PAD, LANES)
    ring_z = nx // RING_X
    hbm = pl.BlockSpec(memory_space=pl.ANY)
    vmem = pl.BlockSpec(memory_space=pltpu.VMEM)
    dma = pltpu.SemaphoreType.DMA
    packed = (2 * NRHS, LANES)
    return pl.pallas_call(
        functools.partial(krylov_kernel, nx, ny),
        out_shape=(
            jax.ShapeDtypeStruct((S + 1, bx, by, NRHS, LANES), F32),
            jax.ShapeDtypeStruct(packed, F32),
        ),
        in_specs=[hbm, hbm, hbm, pl.BlockSpec(memory_space=pltpu.SMEM), vmem],
        out_specs=(hbm, vmem),
        scratch_shapes=[
            pltpu.VMEM((bx, by, LANES), jnp.int32),
            pltpu.VMEM(wide, jnp.int32),
            pltpu.VMEM((3,) + wide, F32),
            pltpu.VMEM(wide, F32),
            pltpu.VMEM(wide, F32),
            pltpu.VMEM((6,) + wide, F32),
        ]
        + [pltpu.VMEM((ex, ey, NRHS, LANES), F32)] * S
        + [
            pltpu.VMEM((bx, by, NRHS, LANES), F32),
            pltpu.VMEM((ROWS, 2 * ROWS), F32),
            pltpu.VMEM((ny,) + packed, F32),
            pltpu.VMEM((RING_X,) + packed, F32),
            pltpu.VMEM((ring_z,) + packed, F32),
            dma((3,)),
            dma((8,)),
            dma((8,)),
            dma(()),
            dma((3,)),
            dma((3,)),
        ],
        compiler_params=pltpu.CompilerParams(
            collective_id=0, has_side_effects=True, vmem_limit_bytes=56 * 2**20
        ),
    )(phase_label, tab_index, source_field, sigma_table, gain)


def combine_call(basis, total):
    bx, by = basis.shape[1], basis.shape[2]
    hbm = pl.BlockSpec(memory_space=pl.ANY)
    vmem = pl.BlockSpec(memory_space=pltpu.VMEM)
    dma = pltpu.SemaphoreType.DMA
    out = jax.ShapeDtypeStruct((NRHS, bx, by, LANES), F32)
    return pl.pallas_call(
        combine_kernel,
        out_shape=(out, out),
        in_specs=[hbm, vmem],
        out_specs=(hbm, hbm),
        scratch_shapes=[
            pltpu.VMEM(basis.shape, F32),
            pltpu.VMEM((bx, NRHS, by + PAD, LANES), F32),
            pltpu.VMEM((bx, NRHS, by + PAD, LANES), F32),
            pltpu.VMEM((4 * NRHS, 2 * LANES), BF16),
            dma((bx // 2,)),
            dma(()),
            dma(()),
        ],
        compiler_params=pltpu.CompilerParams(vmem_limit_bytes=56 * 2**20),
    )(basis, total)


def solution(mesh):
    nx, ny = mesh.shape["gx"], mesh.shape["gy"]

    def shards(phase_label, tab_index, source_field, sigma_table, pattern_gain):
        basis, total = krylov_call(nx, ny, phase_label, tab_index, source_field, sigma_table, pattern_gain)
        return combine_call(basis, total)

    return jax.shard_map(
        shards,
        mesh=mesh,
        in_specs=(P("gx", "gy", None), P("gx", "gy", None), P("gx", "gy", None), P(), P()),
        out_specs=(P(None, "gx", "gy", None), P(None, "gx", "gy", None)),
        check_vma=False,
    )
```

```python
import functools

import jax
import jax.numpy as jnp
from jax import lax
from jax.experimental import pallas as pl
from jax.experimental.pallas import tpu as pltpu
from jax.sharding import PartitionSpec as P

S = 4
NRHS = 16
LANES = 128
PAD = 8
RING_X = 4
MESH = pl.DeviceIdType.MESH
F32 = jnp.float32
BF16 = jnp.bfloat16
ROWS = (S + 1) * NRHS
BASIS = S * NRHS


def split_hi_lo(value):
    high = value.astype(BF16)
    low = (value - high.astype(F32)).astype(BF16)
    return high, low


def lane_pick(table, index):
    numbers = lax.GatherDimensionNumbers(
        offset_dims=(),
        collapsed_slice_dims=(1,),
        start_index_map=(1,),
        operand_batching_dims=(0,),
        start_indices_batching_dims=(0,),
    )
    return lax.gather(
        table, index[..., None], numbers, (1, 1), mode=lax.GatherScatterMode.PROMISE_IN_BOUNDS
    )


def krylov_kernel(nx, ny, phase_hbm, tab_hbm, source_hbm, sigma_ref, gain_ref, basis_hbm, total_ref,
                  phase_own, tab_ext, wide, conduct, charge, weight, f0, f1, f2, f3, f4, p0, p1, p2, acc,
                  part1, part2, part3, own_sem, face_send, face_recv, basis_sem, ring_send, ring_recv):
    bx, by = phase_hbm.shape[0], phase_hbm.shape[1]
    ex = bx + 2 * S
    ey = by + 2 * S
    gx, gy = lax.axis_index("gx"), lax.axis_index("gy")
    xi, zi = lax.rem(gx, RING_X), lax.div(gx, RING_X)
    ring_z = nx // RING_X
    right, left = lax.rem(gx + 1, nx), lax.rem(gx + nx - 1, nx)
    up, down = lax.rem(gy + 1, ny), lax.rem(gy + ny - 1, ny)

    def at_y(o):
        return gx, lax.rem(gy + o, ny)

    def at_x(o):
        return zi * RING_X + lax.rem(xi + o, RING_X), gy

    def at_z(o):
        return lax.rem(zi + o, ring_z) * RING_X + xi, gy

    faces = ((right, gy), (left, gy), (right, up), (right, down), (left, up), (left, down))
    peers = faces + tuple(at_y(o) for o in range(1, ny)) + tuple(at_x(o) for o in range(1, RING_X)) + tuple(
        at_z(o) for o in range(1, ring_z))
    barrier = pltpu.get_barrier_semaphore()
    for peer in peers:
        pl.semaphore_signal(barrier, inc=1, device_id=peer, device_id_type=MESH)

    own = (pl.ds(S, bx), pl.ds(PAD, by))
    own_copies = [
        pltpu.make_async_copy(phase_hbm, phase_own, own_sem.at[0]),
        pltpu.make_async_copy(tab_hbm, tab_ext.at[own], own_sem.at[1]),
        pltpu.make_async_copy(source_hbm, wide.at[(2,) + own], own_sem.at[2]),
    ]
    for copy in own_copies:
        copy.start()
    corner = jnp.zeros((PAD, LANES), F32)
    for a in range(3):
        for x in (0, ex - 1):
            for y in (0, PAD + by):
                wide[a, x, y : y + PAD, :] = corner
    acc[...] = jnp.zeros_like(acc)
    sigma0, sigma1, sigma2 = sigma_ref[0], sigma_ref[1], sigma_ref[2]
    gain = jnp.concatenate([gain_ref[...], jnp.zeros((NRHS, LANES - gain_ref.shape[1]), F32)], axis=1)
    for copy in own_copies:
        copy.wait()

    def fill_row(r, carry):
        phase = phase_own[r]
        value = jnp.where(phase == 0, sigma0, jnp.where(phase == 1, sigma1, sigma2))
        wide[0, r + S, PAD : PAD + by, :] = value
        wide[1, r + S, PAD : PAD + by, :] = tab_ext[r + S, PAD : PAD + by, :].astype(F32)
        return carry

    lax.fori_loop(0, bx, fill_row, 0, unroll=4)
    pl.semaphore_wait(barrier, len(peers))

    x_all, y_all = (0, bx), (0, by)
    x_top, x_low = (bx - S, S), (0, S)
    x_top3, x_low3 = (bx - S + 1, S - 1), (0, S - 1)
    y_top, y_low = (by - PAD, PAD), (0, PAD)
    routes = (
        ((right, gy), x_top, y_all, 0, PAD),
        ((left, gy), x_low, y_all, S + bx, PAD),
        ((gx, up), x_all, y_top, S, 0),
        ((gx, down), x_all, y_low, S, PAD + by),
        ((right, up), x_top3, y_top, 1, 0),
        ((right, down), x_top3, y_low, 1, PAD + by),
        ((left, up), x_low3, y_top, S + bx, 0),
        ((left, down), x_low3, y_low, S + bx, PAD + by),
    )
    face_copies = []
    for r, (peer, xs, ys, dx, dy) in enumerate(routes):
        copy = pltpu.make_async_remote_copy(
            src_ref=wide.at[:, pl.ds(S + xs[0], xs[1]), pl.ds(PAD + ys[0], ys[1])],
            dst_ref=wide.at[:, pl.ds(dx, xs[1]), pl.ds(dy, ys[1])],
            send_sem=face_send.at[r],
            recv_sem=face_recv.at[r],
            device_id=peer,
            device_id_type=MESH,
        )
        copy.start()
        face_copies.append(copy)

    lane = lax.broadcasted_iota(jnp.int32, (PAD * 2 + by, LANES), 1)
    row_y = lax.broadcasted_iota(jnp.int32, (PAD * 2 + by, LANES), 0) + (gy * by - PAD)
    in_y = (row_y >= 0) & (row_y < ny * by)

    fields = (f0, f1, f2, f3)
    pieces = (p0, p1, p2)

    def keep_pieces(m, row, column, value):
        high, low = split_hi_lo(value)
        pieces[m][row, column, :NRHS, :] = high
        pieces[m][row, column, NRHS:, :] = low

    def start_columns(x, columns, strength, row=None):
        for j in columns:
            tab = jnp.broadcast_to(tab_ext[x, pl.ds(j + PAD - S, 1), :], (NRHS, LANES))
            value = lane_pick(gain, tab) * jnp.broadcast_to(strength(j + PAD - S), (NRHS, LANES))
            f0[x, j] = value
            if row is not None:
                keep_pieces(0, row, j - S, value)
            yield

    def start_own(x, carry):
        run(start_columns(x, range(S, S + by), lambda y: wide[2, x, pl.ds(y, 1), :], x - S))
        return carry

    def mask_row(x, sides):
        row_x = gx * bx + x - S
        inside = in_y & (row_x >= 0) & (row_x < nx * bx)
        conduct[x] = jnp.where(inside, wide[0, x], 0.0)
        charge[x] = jnp.where(inside, wide[2, x], 0.0)
        for first, count in sides:
            tab_ext[x, first : first + count, :] = wide[1, x, first : first + count, :].astype(jnp.int32)

    def mask_own(x, carry):
        mask_row(x, ((0, PAD), (PAD + by, PAD)))
        sides = tuple(range(S)) + tuple(range(S + by, ey))
        run(start_columns(x, sides, lambda y: charge[x, pl.ds(y, 1), :]))
        return carry

    def start_far(rows):
        for x in rows:
            mask_row(x, ((0, 2 * PAD + by),))
        for x in rows:
            yield from start_columns(x, range(ey), lambda y, x=x: charge[x, pl.ds(y, 1), :])

    def weight_row(x, carry):
        c = conduct[x]
        zero = jnp.zeros_like(c)
        rows = by + 2 * PAD
        xm = c + conduct[x - 1]
        xp = c + conduct[x + 1]
        ym = c + pltpu.roll(c, 1, 0)
        yp = c + pltpu.roll(c, rows - 1, 0)
        low, top = lane > 0, lane < LANES - 1
        zm = c + jnp.where(low, pltpu.roll(c, 1, 1), zero)
        zp = c + jnp.where(top, pltpu.roll(c, LANES - 1, 1), zero)
        total = ((xm + xp) + (ym + yp)) + (zm + zp)
        inside = c > 0
        inverse = jnp.where(inside, 1.0 / jnp.where(inside, total, 1.0), 0.0)
        weight[0, x] = xm * inverse
        weight[1, x] = xp * inverse
        weight[2, x] = ym * inverse
        weight[3, x] = yp * inverse
        weight[4, x] = jnp.where(low, zm * inverse, zero)
        weight[5, x] = jnp.where(top, zp * inverse, zero)
        return carry

    def mean_rows(src, x, count, columns, store):
        before = [src[x + r, columns[0] - 1] for r in range(count)]
        centre = [src[x + r, columns[0]] for r in range(count)]
        for j in columns:
            after = [src[x + r, j + 1] for r in range(count)]
            edge = [src[x - 1, j]] + centre + [src[x + count, j]]
            for r in range(count):
                w = [jnp.broadcast_to(weight[d, x + r, pl.ds(j + PAD - S, 1), :], (NRHS, LANES)) for d in range(6)]
                value = (w[0] * edge[r] + w[1] * edge[r + 2]) + (w[2] * before[r] + w[3] * after[r])
                value = value + (w[4] * pltpu.roll(centre[r], 1, 1) + w[5] * pltpu.roll(centre[r], LANES - 1, 1))
                store(r, j, value, centre[r])
            before, centre = centre, after
            yield

    def inner_pair(m, x, rows):
        def store(r, j, value, centre):
            fields[m][x + r, j] = value
            if m < S - 1 and rows[r] is not None and S <= j < S + by:
                keep_pieces(m, rows[r], j - S, value)

        return mean_rows(fields[m - 1], x, 2, range(m, ey - m), store)

    def far_pair(m, first, i):
        rows = []
        for r in range(2):
            spots = [first + 2 * k + r - S for k in range(2)]
            inside = [0 <= spot < bx for spot in spots]
            spots = [spot if ok else bx for spot, ok in zip(spots, inside)]
            rows.append(spots[0] + (spots[1] - spots[0]) * i if any(inside) else None)
        return inner_pair(m, first + 2 * i, rows)

    def last_row(x):
        row = x - S
        step = 8
        columns = []

        def store(r, j, value, centre):
            f4[row, j - S] = value
            parts = [split_hi_lo(centre), split_hi_lo(value)]
            highs = [p[row, j - S, :NRHS, :] for p in pieces] + [p[0] for p in parts]
            lows = [p[row, j - S, NRHS:, :] for p in pieces] + [p[1] for p in parts]
            columns.append(jnp.concatenate(highs + lows, axis=0))

        for _ in mean_rows(f3, x, 1, range(S, S + by), store):
            if len(columns) == step:
                block = jnp.concatenate(columns, axis=1)
                acc[...] += lax.dot_general(
                    block[:ROWS], block, (((1,), (1,)), ((), ())), preferred_element_type=F32
                )
                columns.clear()
            yield

    def run(work):
        for _ in work:
            pass

    def weave(work, count, other, extra):
        done = 0
        for k, _ in enumerate(work):
            while done * count < extra * (k + 1):
                next(other, None)
                done += 1
        run(other)

    def rows_of(first, count, body):
        lax.fori_loop(first, first + count, body, 0)

    def pairs_of(m):
        def body(i, carry):
            x = S + m + 2 * i
            run(inner_pair(m, x, (x - S, x + 1 - S)))
            return carry

        lax.fori_loop(0, bx // 2 - m, body, 0)

    def twice(work):
        def body(i, carry):
            work(i)
            return carry

        lax.fori_loop(0, 2, body, 0)

    def keep(m, first, count):
        src = f4.at[pl.ds(first, count)] if m == S else fields[m].at[pl.ds(S + first, count), pl.ds(S, by)]
        pltpu.make_async_copy(src, basis_hbm.at[m, pl.ds(first, count)], basis_sem).start()

    rows_of(S, bx, start_own)
    keep(0, 0, bx)
    for copy in face_copies[2:4]:
        copy.wait_recv()
    rows_of(S, bx, mask_own)
    rows_of(S + 1, bx - 2, weight_row)
    for m in range(1, S):
        pairs_of(m)
        keep(m, m, bx - 2 * m)

    for copy in face_copies[:2] + face_copies[4:]:
        copy.wait_recv()
    low, top, inner = S, bx, 2 * S
    wide_pair = 2 * ey
    twice(lambda i: weave(last_row(inner + i), by, start_far((2 * i, 2 * i + 1)), wide_pair))
    rows_of(1, S, weight_row)
    twice(lambda i: weave(last_row(inner + 2 + i), by, far_pair(1, 1, i), ey - 2))
    twice(lambda i: weave(last_row(inner + 4 + i), by, far_pair(2, 2, i), ey - 4))
    far = S + bx
    twice(lambda i: weave(last_row(inner + 6 + i), by, start_far((far + 2 * i, far + 2 * i + 1)), wide_pair))
    keep(S, S, bx - 2 * S)
    rows_of(far - 1, S, weight_row)
    twice(lambda i: run(far_pair(3, 3, i)))
    twice(lambda i: weave(last_row(low + i), by, far_pair(1, far - 1, i), ey - 2))
    twice(lambda i: weave(last_row(low + 2 + i), by, far_pair(2, far - 2, i), ey - 4))
    keep(S, 0, S)
    twice(lambda i: run(far_pair(3, far - 3, i)))
    for m in range(1, S):
        keep(m, 0, m)
        keep(m, bx - m, m)

    def last_top(x, carry):
        run(last_row(x))
        return carry

    rows_of(top, S, last_top)
    keep(S, bx - S, S)

    both = acc[...]
    lane_g = lax.broadcasted_iota(jnp.int32, (ROWS, LANES), 1)
    first = both[:, :LANES]
    second = jnp.concatenate([both[:, LANES:], jnp.zeros((ROWS, 2 * LANES - 2 * ROWS), F32)], axis=1)
    cross = pltpu.roll(jnp.where(lane_g >= ROWS, first, second), LANES - ROWS, 1)
    cross = jnp.where(lane_g < ROWS, cross, 0.0)
    square = jnp.concatenate([cross, jnp.zeros((LANES - ROWS, LANES), F32)], axis=0)
    gram = jnp.where(lane_g < ROWS, first, 0.0) + cross + square.T[:ROWS]
    lane_b = lane_g[:NRHS]
    blocks = [gram[m * NRHS : (m + 1) * NRHS] for m in range(S + 1)]
    part1[gy, :NRHS] = blocks[0] + jnp.where(lane_b < ROWS, 0.0, pltpu.roll(blocks[2], 48, 1))
    part1[gy, NRHS:] = jnp.where(
        lane_b < ROWS,
        blocks[1],
        jnp.where(lane_b < 112, pltpu.roll(blocks[3], 32, 1), pltpu.roll(blocks[4], 48, 1)),
    )

    sends = []

    def spread(k, peers_of, slots, slot):
        copies = []
        for peer in peers_of:
            copy = pltpu.make_async_remote_copy(
                src_ref=slots.at[slot],
                dst_ref=slots.at[slot],
                send_sem=ring_send.at[k],
                recv_sem=ring_recv.at[k],
                device_id=peer,
                device_id_type=MESH,
            )
            copy.start()
            copies.append(copy)
        others = slots.at[pl.ds(0, len(copies))]
        whole = pltpu.make_async_copy(others, others, ring_recv.at[k])
        whole.wait()
        sends.append(pltpu.make_async_copy(others, others, ring_send.at[k]))
        return jnp.sum(slots[...], axis=0)

    part2[xi] = spread(0, [at_y(o) for o in range(1, ny)], part1, gy)
    part3[zi] = spread(1, [at_x(o) for o in range(1, RING_X)], part2, xi)
    total_ref[...] = spread(2, [at_z(o) for o in range(1, ring_z)], part3, zi)

    for send in sends:
        send.wait()
    for copy in face_copies:
        copy.wait_send()
    pltpu.make_async_copy(basis_hbm, basis_hbm, basis_sem).wait()


def solve_table(total):
    top, low = total[:NRHS], total[NRHS:]
    blocks = [top, low, pltpu.roll(top, 80, 1), pltpu.roll(low, 96, 1), pltpu.roll(low, 80, 1)]
    upper = jnp.concatenate(blocks + [jnp.zeros((LANES - ROWS, LANES), F32)], axis=0)
    lane = lax.broadcasted_iota(jnp.int32, (LANES, LANES), 1)
    row = lax.broadcasted_iota(jnp.int32, (LANES, LANES), 0)
    keep = (lane // NRHS >= row // NRHS) & (lane < ROWS)
    upper = jnp.where(keep, upper, 0.0)
    gram = jnp.where(keep, upper, upper.T)
    down = gram[:BASIS] - gram[NRHS : BASIS + NRHS]
    lane64, row64 = lane[:BASIS], row[:BASIS]
    hess = down - pltpu.roll(down, LANES - NRHS, 1)
    work = jnp.where(lane64 < BASIS, hess, jnp.where(lane64 < ROWS, pltpu.roll(down, BASIS, 1), 0.0))
    for j in range(BASIS):
        pivot = work[j : j + 1, :]
        scaled = pivot / pivot[:, j : j + 1]
        column = work[:, j : j + 1]
        work = jnp.where(row64 == j, scaled, work - column * scaled)
    coeffs = jnp.where(lane64 < NRHS, pltpu.roll(work, LANES - BASIS, 1), 0.0)
    gap = jnp.zeros((NRHS, LANES), F32)
    full = jnp.concatenate([coeffs, gap], axis=0)
    moved = jnp.concatenate([gap, coeffs], axis=0)
    unit = jnp.where((lane[:ROWS] == row[:ROWS]) & (lane[:ROWS] < NRHS), 1.0, 0.0)
    pair = full + pltpu.roll(unit - (full - moved), NRHS, 1)
    tall = jnp.concatenate([pair, pair, jnp.zeros((2 * LANES - 2 * ROWS, LANES), F32)], axis=0)
    return jnp.concatenate([tall[:LANES].T, tall[LANES:].T], axis=1)[: 2 * NRHS]


def combine_kernel(basis_hbm, total_ref, sol_hbm, res_hbm, basis, sol, res, left_ref, basis_sem, sol_sem, res_sem):
    bx, by = basis_hbm.shape[1], basis_hbm.shape[2]
    group = bx // basis_sem.shape[0]
    pitch = sol.shape[2]

    def load(g):
        rows = pl.ds(g * group, group)
        return pltpu.make_async_copy(basis_hbm.at[:, rows], basis.at[:, rows], basis_sem.at[g])

    for g in range(bx // group):
        load(g).start()

    high, low = split_hi_lo(solve_table(total_ref[...]))
    left_ref[...] = jnp.concatenate([high, low], axis=0)
    left = left_ref[:, : 2 * ROWS]

    def combine_row(x):
        for y in range(0, by, 2):
            columns = []
            for k in range(2):
                parts = [split_hi_lo(basis[m, x, y + k]) for m in range(S + 1)]
                columns.append(jnp.concatenate([p[0] for p in parts] + [p[1] for p in parts], axis=0))
            both = jnp.dot(left, jnp.concatenate(columns, axis=1), preferred_element_type=F32)
            both = both[: 2 * NRHS] + both[2 * NRHS :]
            for k in range(2):
                part = both[:, k * LANES : (k + 1) * LANES]
                sol.at[x].reshape(NRHS * pitch, LANES)[pl.ds(y + k, NRHS, stride=pitch), :] = part[:NRHS]
                res.at[x].reshape(NRHS * pitch, LANES)[pl.ds(y + k, NRHS, stride=pitch), :] = part[NRHS:]
        pltpu.make_async_copy(sol.at[x, :, pl.ds(0, by)], sol_hbm.at[:, x], sol_sem).start()
        pltpu.make_async_copy(res.at[x, :, pl.ds(0, by)], res_hbm.at[:, x], res_sem).start()

    def body(g, carry):
        load(g).wait()
        for r in range(group):
            combine_row(g * group + r)
        return carry

    lax.fori_loop(0, bx // group, body, 0)
    pltpu.make_async_copy(sol_hbm, sol_hbm, sol_sem).wait()
    pltpu.make_async_copy(res_hbm, res_hbm, res_sem).wait()


def krylov_call(nx, ny, phase_label, tab_index, source_field, sigma_table, gain):
    bx, by = phase_label.shape[0], phase_label.shape[1]
    ex, ey = bx + 2 * S, by + 2 * S
    wide = (ex, by + 2 * PAD, LANES)
    ring_z = nx // RING_X
    hbm = pl.BlockSpec(memory_space=pl.ANY)
    vmem = pl.BlockSpec(memory_space=pltpu.VMEM)
    dma = pltpu.SemaphoreType.DMA
    packed = (2 * NRHS, LANES)
    return pl.pallas_call(
        functools.partial(krylov_kernel, nx, ny),
        out_shape=(
            jax.ShapeDtypeStruct((S + 1, bx, by, NRHS, LANES), F32),
            jax.ShapeDtypeStruct(packed, F32),
        ),
        in_specs=[hbm, hbm, hbm, pl.BlockSpec(memory_space=pltpu.SMEM), vmem],
        out_specs=(hbm, vmem),
        scratch_shapes=[
            pltpu.VMEM((bx, by, LANES), jnp.int32),
            pltpu.VMEM(wide, jnp.int32),
            pltpu.VMEM((3,) + wide, F32),
            pltpu.VMEM(wide, F32),
            pltpu.VMEM(wide, F32),
            pltpu.VMEM((6,) + wide, F32),
        ]
        + [pltpu.VMEM((ex, ey, NRHS, LANES), F32)] * S
        + [
            pltpu.VMEM((bx, by, NRHS, LANES), F32),
            pltpu.VMEM((bx + 1, by, 2 * NRHS, LANES), BF16),
            pltpu.VMEM((bx + 1, by, 2 * NRHS, LANES), BF16),
            pltpu.VMEM((bx + 1, by, 2 * NRHS, LANES), BF16),
            pltpu.VMEM((ROWS, 2 * ROWS), F32),
            pltpu.VMEM((ny,) + packed, F32),
            pltpu.VMEM((RING_X,) + packed, F32),
            pltpu.VMEM((ring_z,) + packed, F32),
            dma((3,)),
            dma((8,)),
            dma((8,)),
            dma(()),
            dma((3,)),
            dma((3,)),
        ],
        compiler_params=pltpu.CompilerParams(
            collective_id=0, has_side_effects=True, vmem_limit_bytes=60 * 2**20
        ),
    )(phase_label, tab_index, source_field, sigma_table, gain)


def combine_call(basis, total):
    bx, by = basis.shape[1], basis.shape[2]
    hbm = pl.BlockSpec(memory_space=pl.ANY)
    vmem = pl.BlockSpec(memory_space=pltpu.VMEM)
    dma = pltpu.SemaphoreType.DMA
    out = jax.ShapeDtypeStruct((NRHS, bx, by, LANES), F32)
    return pl.pallas_call(
        combine_kernel,
        out_shape=(out, out),
        in_specs=[hbm, vmem],
        out_specs=(hbm, hbm),
        scratch_shapes=[
            pltpu.VMEM(basis.shape, F32),
            pltpu.VMEM((bx, NRHS, by + PAD, LANES), F32),
            pltpu.VMEM((bx, NRHS, by + PAD, LANES), F32),
            pltpu.VMEM((4 * NRHS, 2 * LANES), BF16),
            dma((bx // 2,)),
            dma(()),
            dma(()),
        ],
        compiler_params=pltpu.CompilerParams(vmem_limit_bytes=56 * 2**20),
    )(basis, total)


def solution(mesh):
    nx, ny = mesh.shape["gx"], mesh.shape["gy"]

    def shards(phase_label, tab_index, source_field, sigma_table, pattern_gain):
        basis, total = krylov_call(nx, ny, phase_label, tab_index, source_field, sigma_table, pattern_gain)
        return combine_call(basis, total)

    return jax.shard_map(
        shards,
        mesh=mesh,
        in_specs=(P("gx", "gy", None), P("gx", "gy", None), P("gx", "gy", None), P(), P()),
        out_specs=(P(None, "gx", "gy", None), P(None, "gx", "gy", None)),
        check_vma=False,
    )
```

```python
import functools

import jax
import jax.numpy as jnp
from jax import lax
from jax.experimental import pallas as pl
from jax.experimental.pallas import tpu as pltpu
from jax.sharding import PartitionSpec as P

S = 4
NRHS = 16
LANES = 128
PAD = 8
RING_X = 4
MESH = pl.DeviceIdType.MESH
F32 = jnp.float32
BF16 = jnp.bfloat16
ROWS = (S + 1) * NRHS
BASIS = S * NRHS


def split_hi_lo(value):
    high = value.astype(BF16)
    low = (value - high.astype(F32)).astype(BF16)
    return high, low


def lane_pick(table, index):
    numbers = lax.GatherDimensionNumbers(
        offset_dims=(),
        collapsed_slice_dims=(1,),
        start_index_map=(1,),
        operand_batching_dims=(0,),
        start_indices_batching_dims=(0,),
    )
    return lax.gather(
        table, index[..., None], numbers, (1, 1), mode=lax.GatherScatterMode.PROMISE_IN_BOUNDS
    )


def krylov_kernel(nx, ny, phase_hbm, tab_hbm, source_hbm, sigma_ref, gain_ref, basis_hbm, total_ref,
                  phase_own, tab_ext, wide, conduct, charge, weight, f0, f1, f2, f3, f4, p0, p1, p2, acc,
                  part1, part2, part3, own_sem, face_send, face_recv, basis_sem, ring_send, ring_recv):
    bx, by = phase_hbm.shape[0], phase_hbm.shape[1]
    ex = bx + 2 * S
    ey = by + 2 * S
    gx, gy = lax.axis_index("gx"), lax.axis_index("gy")
    xi, zi = lax.rem(gx, RING_X), lax.div(gx, RING_X)
    ring_z = nx // RING_X
    right, left = lax.rem(gx + 1, nx), lax.rem(gx + nx - 1, nx)
    up, down = lax.rem(gy + 1, ny), lax.rem(gy + ny - 1, ny)

    def at_y(o):
        return gx, lax.rem(gy + o, ny)

    def at_x(o):
        return zi * RING_X + lax.rem(xi + o, RING_X), gy

    def at_z(o):
        return lax.rem(zi + o, ring_z) * RING_X + xi, gy

    own = (pl.ds(S, bx), pl.ds(PAD, by))
    own_copies = [
        pltpu.make_async_copy(phase_hbm, phase_own, own_sem.at[0]),
        pltpu.make_async_copy(tab_hbm, tab_ext.at[own], own_sem.at[1]),
        pltpu.make_async_copy(source_hbm, wide.at[(2,) + own], own_sem.at[2]),
    ]
    for copy in own_copies:
        copy.start()
    faces = ((right, gy), (left, gy), (right, up), (right, down), (left, up), (left, down))
    peers = faces + tuple(at_y(o) for o in range(1, ny)) + tuple(at_x(o) for o in range(1, RING_X)) + tuple(
        at_z(o) for o in range(1, ring_z))
    barrier = pltpu.get_barrier_semaphore()
    for peer in peers:
        pl.semaphore_signal(barrier, inc=1, device_id=peer, device_id_type=MESH)
    corner = jnp.zeros((PAD, LANES), F32)
    for a in range(3):
        for x in (0, ex - 1):
            for y in (0, PAD + by):
                wide[a, x, y : y + PAD, :] = corner
    acc[...] = jnp.zeros_like(acc)
    sigma0, sigma1, sigma2 = sigma_ref[0], sigma_ref[1], sigma_ref[2]
    gain = jnp.concatenate([gain_ref[...], jnp.zeros((NRHS, LANES - gain_ref.shape[1]), F32)], axis=1)
    for copy in own_copies:
        copy.wait()

    def fill_row(r, carry):
        phase = phase_own[r]
        value = jnp.where(phase == 0, sigma0, jnp.where(phase == 1, sigma1, sigma2))
        wide[0, r + S, PAD : PAD + by, :] = value
        conduct[r + S, PAD : PAD + by, :] = value
        wide[1, r + S, PAD : PAD + by, :] = tab_ext[r + S, PAD : PAD + by, :].astype(F32)
        return carry

    lax.fori_loop(0, bx, fill_row, 0, unroll=4)
    lane = lax.broadcasted_iota(jnp.int32, (PAD * 2 + by, LANES), 1)
    row_y = lax.broadcasted_iota(jnp.int32, (PAD * 2 + by, LANES), 0) + (gy * by - PAD)
    in_y = (row_y >= 0) & (row_y < ny * by)

    fields = (f0, f1, f2, f3)
    pieces = (p0, p1, p2)

    def keep_pieces(m, row, column, value):
        high, low = split_hi_lo(value)
        pieces[m][row, column, :NRHS, :] = high
        pieces[m][row, column, NRHS:, :] = low

    def start_columns(x, columns, strength, row=None):
        for j in columns:
            tab = jnp.broadcast_to(tab_ext[x, pl.ds(j + PAD - S, 1), :], (NRHS, LANES))
            value = lane_pick(gain, tab) * jnp.broadcast_to(strength(j + PAD - S), (NRHS, LANES))
            f0[x, j] = value
            if row is not None:
                keep_pieces(0, row, j - S, value)
            yield

    def start_own(x, carry):
        run(start_columns(x, range(S, S + by), lambda y: wide[2, x, pl.ds(y, 1), :], x - S))
        return carry

    def mask_row(x, sides):
        row_x = gx * bx + x - S
        in_x = (row_x >= 0) & (row_x < nx * bx)
        for first, count in sides:
            at = slice(first, first + count)
            inside = in_y[at] & in_x
            conduct[x, at, :] = jnp.where(inside, wide[0, x, at, :], 0.0)
            charge[x, at, :] = jnp.where(inside, wide[2, x, at, :], 0.0)
            tab_ext[x, at, :] = wide[1, x, at, :].astype(jnp.int32)

    def mask_own(x, carry):
        mask_row(x, ((0, PAD), (PAD + by, PAD)))
        sides = tuple(range(S)) + tuple(range(S + by, ey))
        run(start_columns(x, sides, lambda y: charge[x, pl.ds(y, 1), :]))
        return carry

    def start_far(rows):
        for x in rows:
            mask_row(x, ((0, 2 * PAD + by),))
        for x in rows:
            yield from start_columns(x, range(ey), lambda y, x=x: charge[x, pl.ds(y, 1), :])

    def weight_part(x, first, count, start, stop):
        at = slice(first, first + count)
        c = conduct[x, at, :]
        zero = jnp.zeros_like(c)
        xm = c + conduct[x - 1, at, :]
        xp = c + conduct[x + 1, at, :]
        ym = c + pltpu.roll(c, 1, 0)
        yp = c + pltpu.roll(c, count - 1, 0)
        low, top = lane[at] > 0, lane[at] < LANES - 1
        zm = c + jnp.where(low, pltpu.roll(c, 1, 1), zero)
        zp = c + jnp.where(top, pltpu.roll(c, LANES - 1, 1), zero)
        total = ((xm + xp) + (ym + yp)) + (zm + zp)
        inside = c > 0
        inverse = jnp.where(inside, 1.0 / jnp.where(inside, total, 1.0), 0.0)
        parts = (xm, xp, ym, yp, jnp.where(low, zm, zero), jnp.where(top, zp, zero))
        for d, part in enumerate(parts):
            weight[d, x, start:stop, :] = (part * inverse)[start - first : stop - first]

    def weight_row(x, carry):
        weight_part(x, 0, by + 2 * PAD, 0, by + 2 * PAD)
        return carry

    def weight_inner(x, carry):
        weight_part(x, PAD, by, PAD, PAD + by)
        return carry

    def weight_sides(x, carry):
        weight_part(x, 0, 2 * PAD, 0, PAD + 1)
        weight_part(x, by, 2 * PAD, PAD + by - 1, by + 2 * PAD)
        return carry

    def mean_rows(src, x, count, columns, store):
        before = [src[x + r, columns[0] - 1] for r in range(count)]
        centre = [src[x + r, columns[0]] for r in range(count)]
        for j in columns:
            after = [src[x + r, j + 1] for r in range(count)]
            edge = [src[x - 1, j]] + centre + [src[x + count, j]]
            for r in range(count):
                w = [jnp.broadcast_to(weight[d, x + r, pl.ds(j + PAD - S, 1), :], (NRHS, LANES)) for d in range(6)]
                value = (w[0] * edge[r] + w[1] * edge[r + 2]) + (w[2] * before[r] + w[3] * after[r])
                value = value + (w[4] * pltpu.roll(centre[r], 1, 1) + w[5] * pltpu.roll(centre[r], LANES - 1, 1))
                store(r, j, value, centre[r])
            before, centre = centre, after
            yield

    def inner_pair(m, x, rows, columns=None):
        def store(r, j, value, centre):
            fields[m][x + r, j] = value
            if m < S - 1 and rows[r] is not None and S <= j < S + by:
                keep_pieces(m, rows[r], j - S, value)

        return mean_rows(fields[m - 1], x, 2, range(m, ey - m) if columns is None else columns, store)

    def far_pair(m, first, i):
        rows = []
        for r in range(2):
            spots = [first + 2 * k + r - S for k in range(2)]
            inside = [0 <= spot < bx for spot in spots]
            spots = [spot if ok else bx for spot, ok in zip(spots, inside)]
            rows.append(spots[0] + (spots[1] - spots[0]) * i if any(inside) else None)
        return inner_pair(m, first + 2 * i, rows)

    def last_row(x):
        row = x - S
        step = 8
        columns = []

        def store(r, j, value, centre):
            f4[row, j - S] = value
            parts = [split_hi_lo(centre), split_hi_lo(value)]
            highs = [p[row, j - S, :NRHS, :] for p in pieces] + [p[0] for p in parts]
            lows = [p[row, j - S, NRHS:, :] for p in pieces] + [p[1] for p in parts]
            columns.append(jnp.concatenate(highs + lows, axis=0))

        for _ in mean_rows(f3, x, 1, range(S, S + by), store):
            if len(columns) == step:
                block = jnp.concatenate(columns, axis=1)
                acc[...] += lax.dot_general(
                    block[:ROWS], block, (((1,), (1,)), ((), ())), preferred_element_type=F32
                )
                columns.clear()
            yield

    def run(work):
        for _ in work:
            pass

    def weave(work, count, other, extra):
        done = 0
        for k, _ in enumerate(work):
            while done * count < extra * (k + 1):
                next(other, None)
                done += 1
        run(other)

    def rows_of(first, count, body):
        lax.fori_loop(first, first + count, body, 0, unroll=2)

    def pairs_of(m, *parts):
        def body(i, carry):
            x = S + m + 2 * i
            for columns in parts:
                run(inner_pair(m, x, (x - S, x + 1 - S), columns))
            return carry

        lax.fori_loop(0, bx // 2 - m, body, 0)

    def twice(work):
        def body(i, carry):
            work(i)
            return carry

        lax.fori_loop(0, 2, body, 0)

    def keep(m, first, count):
        src = f4.at[pl.ds(first, count)] if m == S else fields[m].at[pl.ds(S + first, count), pl.ds(S, by)]
        pltpu.make_async_copy(src, basis_hbm.at[m, pl.ds(first, count)], basis_sem).start()

    rows_of(S, bx, start_own)
    pl.semaphore_wait(barrier, len(peers))

    x_all, y_all = (0, bx), (0, by)
    x_top, x_low = (bx - S, S), (0, S)
    x_top3, x_low3 = (bx - S + 1, S - 1), (0, S - 1)
    y_top, y_low = (by - PAD, PAD), (0, PAD)
    routes = (
        ((right, gy), x_top, y_all, 0, PAD),
        ((left, gy), x_low, y_all, S + bx, PAD),
        ((gx, up), x_all, y_top, S, 0),
        ((gx, down), x_all, y_low, S, PAD + by),
        ((right, up), x_top3, y_top, 1, 0),
        ((right, down), x_top3, y_low, 1, PAD + by),
        ((left, up), x_low3, y_top, S + bx, 0),
        ((left, down), x_low3, y_low, S + bx, PAD + by),
    )
    face_copies = []
    for r, (peer, xs, ys, dx, dy) in enumerate(routes):
        copy = pltpu.make_async_remote_copy(
            src_ref=wide.at[:, pl.ds(S + xs[0], xs[1]), pl.ds(PAD + ys[0], ys[1])],
            dst_ref=wide.at[:, pl.ds(dx, xs[1]), pl.ds(dy, ys[1])],
            send_sem=face_send.at[r],
            recv_sem=face_recv.at[r],
            device_id=peer,
            device_id_type=MESH,
        )
        copy.start()
        face_copies.append(copy)
    keep(0, 0, bx)
    rows_of(S + 1, bx - 2, weight_inner)
    pairs_of(1, range(S + 1, S + by - 1))
    for copy in face_copies[2:4]:
        copy.wait_recv()
    rows_of(S, bx, mask_own)
    rows_of(S + 1, bx - 2, weight_sides)
    pairs_of(1, range(1, S + 1), range(S + by - 1, ey - 1))
    keep(1, 1, bx - 2)
    for m in range(2, S):
        pairs_of(m, None)
        keep(m, m, bx - 2 * m)

    for copy in face_copies[:2] + face_copies[4:]:
        copy.wait_recv()
    low, top, inner = S, bx, 2 * S
    wide_pair = 2 * ey
    twice(lambda i: weave(last_row(inner + i), by, start_far((2 * i, 2 * i + 1)), wide_pair))
    rows_of(1, S, weight_row)
    twice(lambda i: weave(last_row(inner + 2 + i), by, far_pair(1, 1, i), ey - 2))
    twice(lambda i: weave(last_row(inner + 4 + i), by, far_pair(2, 2, i), ey - 4))
    far = S + bx
    twice(lambda i: weave(last_row(inner + 6 + i), by, start_far((far + 2 * i, far + 2 * i + 1)), wide_pair))
    keep(S, S, bx - 2 * S)
    rows_of(far - 1, S, weight_row)
    twice(lambda i: run(far_pair(3, 3, i)))
    twice(lambda i: weave(last_row(low + i), by, far_pair(1, far - 1, i), ey - 2))
    twice(lambda i: weave(last_row(low + 2 + i), by, far_pair(2, far - 2, i), ey - 4))
    keep(S, 0, S)
    twice(lambda i: run(far_pair(3, far - 3, i)))
    for m in range(1, S):
        keep(m, 0, m)
        keep(m, bx - m, m)

    def last_top(x, carry):
        run(last_row(x))
        return carry

    lax.fori_loop(top, top + S, last_top, 0)
    keep(S, bx - S, S)

    both = acc[...]
    lane_g = lax.broadcasted_iota(jnp.int32, (ROWS, LANES), 1)
    first = both[:, :LANES]
    second = jnp.concatenate([both[:, LANES:], jnp.zeros((ROWS, 2 * LANES - 2 * ROWS), F32)], axis=1)
    cross = pltpu.roll(jnp.where(lane_g >= ROWS, first, second), LANES - ROWS, 1)
    cross = jnp.where(lane_g < ROWS, cross, 0.0)
    square = jnp.concatenate([cross, jnp.zeros((LANES - ROWS, LANES), F32)], axis=0)
    gram = jnp.where(lane_g < ROWS, first, 0.0) + cross + square.T[:ROWS]
    lane_b = lane_g[:NRHS]
    blocks = [gram[m * NRHS : (m + 1) * NRHS] for m in range(S + 1)]
    part1[gy, :NRHS] = blocks[0] + jnp.where(lane_b < ROWS, 0.0, pltpu.roll(blocks[2], 48, 1))
    part1[gy, NRHS:] = jnp.where(
        lane_b < ROWS,
        blocks[1],
        jnp.where(lane_b < 112, pltpu.roll(blocks[3], 32, 1), pltpu.roll(blocks[4], 48, 1)),
    )

    sends = []

    def spread(k, peers_of, slots, slot):
        copies = []
        for peer in peers_of:
            copy = pltpu.make_async_remote_copy(
                src_ref=slots.at[slot],
                dst_ref=slots.at[slot],
                send_sem=ring_send.at[k],
                recv_sem=ring_recv.at[k],
                device_id=peer,
                device_id_type=MESH,
            )
            copy.start()
            copies.append(copy)
        others = slots.at[pl.ds(0, len(copies))]
        whole = pltpu.make_async_copy(others, others, ring_recv.at[k])
        whole.wait()
        sends.append(pltpu.make_async_copy(others, others, ring_send.at[k]))
        return jnp.sum(slots[...], axis=0)

    part2[xi] = spread(0, [at_y(o) for o in range(1, ny)], part1, gy)
    part3[zi] = spread(1, [at_x(o) for o in range(1, RING_X)], part2, xi)
    total_ref[...] = spread(2, [at_z(o) for o in range(1, ring_z)], part3, zi)

    for send in sends:
        send.wait()
    for copy in face_copies:
        copy.wait_send()
    pltpu.make_async_copy(basis_hbm, basis_hbm, basis_sem).wait()


def solve_table(total):
    top, low = total[:NRHS], total[NRHS:]
    blocks = [top, low, pltpu.roll(top, 80, 1), pltpu.roll(low, 96, 1), pltpu.roll(low, 80, 1)]
    upper = jnp.concatenate(blocks + [jnp.zeros((LANES - ROWS, LANES), F32)], axis=0)
    lane = lax.broadcasted_iota(jnp.int32, (LANES, LANES), 1)
    row = lax.broadcasted_iota(jnp.int32, (LANES, LANES), 0)
    keep = (lane // NRHS >= row // NRHS) & (lane < ROWS)
    upper = jnp.where(keep, upper, 0.0)
    gram = jnp.where(keep, upper, upper.T)
    down = gram[:BASIS] - gram[NRHS : BASIS + NRHS]
    lane64, row64 = lane[:BASIS], row[:BASIS]
    hess = down - pltpu.roll(down, LANES - NRHS, 1)
    work = jnp.where(lane64 < BASIS, hess, jnp.where(lane64 < ROWS, pltpu.roll(down, BASIS, 1), 0.0))
    for j in range(BASIS):
        pivot = work[j : j + 1, :]
        scaled = pivot / pivot[:, j : j + 1]
        column = work[:, j : j + 1]
        work = jnp.where(row64 == j, scaled, work - column * scaled)
    coeffs = jnp.where(lane64 < NRHS, pltpu.roll(work, LANES - BASIS, 1), 0.0)
    gap = jnp.zeros((NRHS, LANES), F32)
    full = jnp.concatenate([coeffs, gap], axis=0)
    moved = jnp.concatenate([gap, coeffs], axis=0)
    unit = jnp.where((lane[:ROWS] == row[:ROWS]) & (lane[:ROWS] < NRHS), 1.0, 0.0)
    pair = full + pltpu.roll(unit - (full - moved), NRHS, 1)
    tall = jnp.concatenate([pair, pair, jnp.zeros((2 * LANES - 2 * ROWS, LANES), F32)], axis=0)
    return jnp.concatenate([tall[:LANES].T, tall[LANES:].T], axis=1)[: 2 * NRHS]


def combine_kernel(basis_hbm, total_ref, sol_hbm, res_hbm, basis, sol, res, left_ref, basis_sem, sol_sem, res_sem):
    bx, by = basis_hbm.shape[1], basis_hbm.shape[2]
    group = bx // basis_sem.shape[0]
    pitch = sol.shape[2]

    def load(g):
        rows = pl.ds(g * group, group)
        return pltpu.make_async_copy(basis_hbm.at[:, rows], basis.at[:, rows], basis_sem.at[g])

    for g in range(bx // group):
        load(g).start()

    high, low = split_hi_lo(solve_table(total_ref[...]))
    left_ref[...] = jnp.concatenate([high, low], axis=0)
    left = left_ref[:, : 2 * ROWS]

    def combine_row(x):
        for y in range(0, by, 2):
            columns = []
            for k in range(2):
                parts = [split_hi_lo(basis[m, x, y + k]) for m in range(S + 1)]
                columns.append(jnp.concatenate([p[0] for p in parts] + [p[1] for p in parts], axis=0))
            both = jnp.dot(left, jnp.concatenate(columns, axis=1), preferred_element_type=F32)
            both = both[: 2 * NRHS] + both[2 * NRHS :]
            for k in range(2):
                part = both[:, k * LANES : (k + 1) * LANES]
                sol.at[x].reshape(NRHS * pitch, LANES)[pl.ds(y + k, NRHS, stride=pitch), :] = part[:NRHS]
                res.at[x].reshape(NRHS * pitch, LANES)[pl.ds(y + k, NRHS, stride=pitch), :] = part[NRHS:]
        pltpu.make_async_copy(sol.at[x, :, pl.ds(0, by)], sol_hbm.at[:, x], sol_sem).start()
        pltpu.make_async_copy(res.at[x, :, pl.ds(0, by)], res_hbm.at[:, x], res_sem).start()

    def body(g, carry):
        load(g).wait()
        for r in range(group):
            combine_row(g * group + r)
        return carry

    lax.fori_loop(0, bx // group, body, 0)
    pltpu.make_async_copy(sol_hbm, sol_hbm, sol_sem).wait()
    pltpu.make_async_copy(res_hbm, res_hbm, res_sem).wait()


def krylov_call(nx, ny, phase_label, tab_index, source_field, sigma_table, gain):
    bx, by = phase_label.shape[0], phase_label.shape[1]
    ex, ey = bx + 2 * S, by + 2 * S
    wide = (ex, by + 2 * PAD, LANES)
    ring_z = nx // RING_X
    hbm = pl.BlockSpec(memory_space=pl.ANY)
    vmem = pl.BlockSpec(memory_space=pltpu.VMEM)
    dma = pltpu.SemaphoreType.DMA
    packed = (2 * NRHS, LANES)
    return pl.pallas_call(
        functools.partial(krylov_kernel, nx, ny),
        out_shape=(
            jax.ShapeDtypeStruct((S + 1, bx, by, NRHS, LANES), F32),
            jax.ShapeDtypeStruct(packed, F32),
        ),
        in_specs=[hbm, hbm, hbm, pl.BlockSpec(memory_space=pltpu.SMEM), vmem],
        out_specs=(hbm, vmem),
        scratch_shapes=[
            pltpu.VMEM((bx, by, LANES), jnp.int32),
            pltpu.VMEM(wide, jnp.int32),
            pltpu.VMEM((3,) + wide, F32),
            pltpu.VMEM(wide, F32),
            pltpu.VMEM(wide, F32),
            pltpu.VMEM((6,) + wide, F32),
        ]
        + [pltpu.VMEM((ex, ey, NRHS, LANES), F32)] * S
        + [
            pltpu.VMEM((bx, by, NRHS, LANES), F32),
            pltpu.VMEM((bx + 1, by, 2 * NRHS, LANES), BF16),
            pltpu.VMEM((bx + 1, by, 2 * NRHS, LANES), BF16),
            pltpu.VMEM((bx + 1, by, 2 * NRHS, LANES), BF16),
            pltpu.VMEM((ROWS, 2 * ROWS), F32),
            pltpu.VMEM((ny,) + packed, F32),
            pltpu.VMEM((RING_X,) + packed, F32),
            pltpu.VMEM((ring_z,) + packed, F32),
            dma((3,)),
            dma((8,)),
            dma((8,)),
            dma(()),
            dma((3,)),
            dma((3,)),
        ],
        compiler_params=pltpu.CompilerParams(
            collective_id=0, has_side_effects=True, vmem_limit_bytes=60 * 2**20
        ),
    )(phase_label, tab_index, source_field, sigma_table, gain)


def combine_call(basis, total):
    bx, by = basis.shape[1], basis.shape[2]
    hbm = pl.BlockSpec(memory_space=pl.ANY)
    vmem = pl.BlockSpec(memory_space=pltpu.VMEM)
    dma = pltpu.SemaphoreType.DMA
    out = jax.ShapeDtypeStruct((NRHS, bx, by, LANES), F32)
    return pl.pallas_call(
        combine_kernel,
        out_shape=(out, out),
        in_specs=[hbm, vmem],
        out_specs=(hbm, hbm),
        scratch_shapes=[
            pltpu.VMEM(basis.shape, F32),
            pltpu.VMEM((bx, NRHS, by + PAD, LANES), F32),
            pltpu.VMEM((bx, NRHS, by + PAD, LANES), F32),
            pltpu.VMEM((4 * NRHS, 2 * LANES), BF16),
            dma((bx // 2,)),
            dma(()),
            dma(()),
        ],
        compiler_params=pltpu.CompilerParams(vmem_limit_bytes=56 * 2**20),
    )(basis, total)


def solution(mesh):
    nx, ny = mesh.shape["gx"], mesh.shape["gy"]

    def shards(phase_label, tab_index, source_field, sigma_table, pattern_gain):
        basis, total = krylov_call(nx, ny, phase_label, tab_index, source_field, sigma_table, pattern_gain)
        return combine_call(basis, total)

    return jax.shard_map(
        shards,
        mesh=mesh,
        in_specs=(P("gx", "gy", None), P("gx", "gy", None), P("gx", "gy", None), P(), P()),
        out_specs=(P(None, "gx", "gy", None), P(None, "gx", "gy", None)),
        check_vma=False,
    )
```

```python
import functools

import jax
import jax.numpy as jnp
from jax import lax
from jax.experimental import pallas as pl
from jax.experimental.pallas import tpu as pltpu
from jax.sharding import PartitionSpec as P

S = 4
NRHS = 16
LANES = 128
PAD = 8
RING_X = 4
MESH = pl.DeviceIdType.MESH
F32 = jnp.float32
BF16 = jnp.bfloat16
ROWS = (S + 1) * NRHS
BASIS = S * NRHS


def split_hi_lo(value):
    high = value.astype(BF16)
    low = (value - high.astype(F32)).astype(BF16)
    return high, low


def lane_pick(table, index):
    numbers = lax.GatherDimensionNumbers(
        offset_dims=(),
        collapsed_slice_dims=(1,),
        start_index_map=(1,),
        operand_batching_dims=(0,),
        start_indices_batching_dims=(0,),
    )
    return lax.gather(
        table, index[..., None], numbers, (1, 1), mode=lax.GatherScatterMode.PROMISE_IN_BOUNDS
    )


def krylov_kernel(nx, ny, phase_hbm, tab_hbm, source_hbm, sigma_hbm, gain_hbm, basis_hbm, total_ref,
                  sigma_ref, gain_ref, phase_own, tab_ext, wide, conduct, charge, weight, f0, f1, f2, f3, f4, p0, p1, p2, acc,
                  part1, part2, part3, own_sem, face_send, face_recv, basis_sem, ring_send, ring_recv):
    bx, by = phase_hbm.shape[0], phase_hbm.shape[1]
    ex = bx + 2 * S
    ey = by + 2 * S
    gx, gy = lax.axis_index("gx"), lax.axis_index("gy")
    xi, zi = lax.rem(gx, RING_X), lax.div(gx, RING_X)
    ring_z = nx // RING_X
    right, left = lax.rem(gx + 1, nx), lax.rem(gx + nx - 1, nx)
    up, down = lax.rem(gy + 1, ny), lax.rem(gy + ny - 1, ny)

    def at_y(o):
        return gx, lax.rem(gy + o, ny)

    def at_x(o):
        return zi * RING_X + lax.rem(xi + o, RING_X), gy

    def at_z(o):
        return lax.rem(zi + o, ring_z) * RING_X + xi, gy

    own = (pl.ds(S, bx), pl.ds(PAD, by))
    own_copies = [
        pltpu.make_async_copy(phase_hbm, phase_own, own_sem.at[0]),
        pltpu.make_async_copy(tab_hbm, tab_ext.at[own], own_sem.at[1]),
        pltpu.make_async_copy(source_hbm, wide.at[(2,) + own], own_sem.at[2]),
        pltpu.make_async_copy(sigma_hbm, sigma_ref, own_sem.at[3]),
        pltpu.make_async_copy(gain_hbm, gain_ref, own_sem.at[4]),
    ]
    for copy in own_copies:
        copy.start()
    faces = ((right, gy), (left, gy), (right, up), (right, down), (left, up), (left, down))
    peers = faces + tuple(at_y(o) for o in range(1, ny)) + tuple(at_x(o) for o in range(1, RING_X)) + tuple(
        at_z(o) for o in range(1, ring_z))
    barrier = pltpu.get_barrier_semaphore()
    for peer in peers:
        pl.semaphore_signal(barrier, inc=1, device_id=peer, device_id_type=MESH)
    corner = jnp.zeros((PAD, LANES), F32)
    for a in range(3):
        for x in (0, ex - 1):
            for y in (0, PAD + by):
                wide[a, x, y : y + PAD, :] = corner
    acc[...] = jnp.zeros_like(acc)
    for copy in own_copies:
        copy.wait()
    sigma0, sigma1, sigma2 = sigma_ref[0], sigma_ref[1], sigma_ref[2]
    gain = jnp.concatenate([gain_ref[...], jnp.zeros((NRHS, LANES - gain_ref.shape[1]), F32)], axis=1)

    def fill_row(r, carry):
        phase = phase_own[r]
        value = jnp.where(phase == 0, sigma0, jnp.where(phase == 1, sigma1, sigma2))
        wide[0, r + S, PAD : PAD + by, :] = value
        conduct[r + S, PAD : PAD + by, :] = value
        wide[1, r + S, PAD : PAD + by, :] = tab_ext[r + S, PAD : PAD + by, :].astype(F32)
        return carry

    lax.fori_loop(0, bx, fill_row, 0, unroll=4)
    lane = lax.broadcasted_iota(jnp.int32, (PAD * 2 + by, LANES), 1)
    row_y = lax.broadcasted_iota(jnp.int32, (PAD * 2 + by, LANES), 0) + (gy * by - PAD)
    in_y = (row_y >= 0) & (row_y < ny * by)

    fields = (f0, f1, f2, f3)
    pieces = (p0, p1, p2)

    def keep_pieces(m, row, column, value):
        high, low = split_hi_lo(value)
        pieces[m][row, column, :NRHS, :] = high
        pieces[m][row, column, NRHS:, :] = low

    def start_columns(x, columns, strength, row=None):
        for j in columns:
            tab = jnp.broadcast_to(tab_ext[x, pl.ds(j + PAD - S, 1), :], (NRHS, LANES))
            value = lane_pick(gain, tab) * jnp.broadcast_to(strength(j + PAD - S), (NRHS, LANES))
            f0[x, j] = value
            if row is not None:
                keep_pieces(0, row, j - S, value)
            yield

    tabs = gain_ref.shape[1]
    rest = gain_ref[...]
    gain_parts = []
    for _ in range(3):
        gain_parts.append(rest.astype(BF16))
        rest = rest - gain_parts[-1].astype(F32)
    gain_stack = jnp.concatenate(gain_parts, axis=0)
    tab_row = lax.broadcasted_iota(jnp.int32, (tabs, LANES), 0)

    def start_pairs(x, columns, strength, row=None):
        for k in range(0, len(columns), 2):
            pair = columns[k : k + 2]
            picks = []
            for j in pair:
                tab = jnp.broadcast_to(tab_ext[x, pl.ds(j + PAD - S, 1), :], (tabs, LANES))
                picks.append(jnp.where(tab == tab_row, 1.0, 0.0).astype(BF16))
            parts = jnp.dot(gain_stack, jnp.concatenate(picks, axis=1), preferred_element_type=F32)
            picked = parts[:NRHS] + (parts[NRHS : 2 * NRHS] + parts[2 * NRHS :])
            for n, j in enumerate(pair):
                value = picked[:, n * LANES : (n + 1) * LANES]
                value = value * jnp.broadcast_to(strength(j + PAD - S), (NRHS, LANES))
                f0[x, j] = value
                if row is not None:
                    keep_pieces(0, row, j - S, value)
            yield

    def start_own(x, carry):
        def strength(y):
            return wide[2, x, pl.ds(y, 1), :]

        split = S + 16
        weave(
            start_columns(x, range(S, split), strength, x - S),
            16,
            start_pairs(x, range(split, S + by), strength, x - S),
            (by - 16) // 2,
        )
        return carry

    def mask_row(x, sides):
        row_x = gx * bx + x - S
        in_x = (row_x >= 0) & (row_x < nx * bx)
        for first, count in sides:
            at = slice(first, first + count)
            inside = in_y[at] & in_x
            conduct[x, at, :] = jnp.where(inside, wide[0, x, at, :], 0.0)
            charge[x, at, :] = jnp.where(inside, wide[2, x, at, :], 0.0)
            tab_ext[x, at, :] = wide[1, x, at, :].astype(jnp.int32)

    def mask_own(x, carry):
        mask_row(x, ((0, PAD), (PAD + by, PAD)))

        def strength(y):
            return charge[x, pl.ds(y, 1), :]

        weave(
            start_columns(x, range(S), strength), S, start_pairs(x, range(S + by, ey), strength), S // 2
        )
        return carry

    def start_far(rows):
        for x in rows:
            mask_row(x, ((0, 2 * PAD + by),))
        for x in rows:
            yield from start_columns(x, range(ey), lambda y, x=x: charge[x, pl.ds(y, 1), :])

    def weight_part(x, first, count, start, stop):
        at = slice(first, first + count)
        c = conduct[x, at, :]
        zero = jnp.zeros_like(c)
        xm = c + conduct[x - 1, at, :]
        xp = c + conduct[x + 1, at, :]
        ym = c + pltpu.roll(c, 1, 0)
        yp = c + pltpu.roll(c, count - 1, 0)
        low, top = lane[at] > 0, lane[at] < LANES - 1
        zm = c + jnp.where(low, pltpu.roll(c, 1, 1), zero)
        zp = c + jnp.where(top, pltpu.roll(c, LANES - 1, 1), zero)
        total = ((xm + xp) + (ym + yp)) + (zm + zp)
        inside = c > 0
        inverse = jnp.where(inside, 1.0 / jnp.where(inside, total, 1.0), 0.0)
        parts = (xm, xp, ym, yp, jnp.where(low, zm, zero), jnp.where(top, zp, zero))
        for d, part in enumerate(parts):
            weight[d, x, start:stop, :] = (part * inverse)[start - first : stop - first]

    def weight_row(x, carry):
        weight_part(x, 0, by + 2 * PAD, 0, by + 2 * PAD)
        return carry

    def weight_inner(x, carry):
        weight_part(x, PAD, by, PAD, PAD + by)
        return carry

    def weight_sides(x, carry):
        weight_part(x, 0, 2 * PAD, 0, PAD + 1)
        weight_part(x, by, 2 * PAD, PAD + by - 1, by + 2 * PAD)
        return carry

    def mean_rows(src, x, count, columns, store):
        before = [src[x + r, columns[0] - 1] for r in range(count)]
        centre = [src[x + r, columns[0]] for r in range(count)]
        for j in columns:
            after = [src[x + r, j + 1] for r in range(count)]
            edge = [src[x - 1, j]] + centre + [src[x + count, j]]
            for r in range(count):
                w = [jnp.broadcast_to(weight[d, x + r, pl.ds(j + PAD - S, 1), :], (NRHS, LANES)) for d in range(6)]
                value = (w[0] * edge[r] + w[1] * edge[r + 2]) + (w[2] * before[r] + w[3] * after[r])
                value = value + (w[4] * pltpu.roll(centre[r], 1, 1) + w[5] * pltpu.roll(centre[r], LANES - 1, 1))
                store(r, j, value, centre[r])
            before, centre = centre, after
            yield

    def inner_pair(m, x, rows, columns=None):
        def store(r, j, value, centre):
            fields[m][x + r, j] = value
            if m < S - 1 and rows[r] is not None and S <= j < S + by:
                keep_pieces(m, rows[r], j - S, value)

        return mean_rows(fields[m - 1], x, 2, range(m, ey - m) if columns is None else columns, store)

    def far_pair(m, first, i):
        rows = []
        for r in range(2):
            spots = [first + 2 * k + r - S for k in range(2)]
            inside = [0 <= spot < bx for spot in spots]
            spots = [spot if ok else bx for spot, ok in zip(spots, inside)]
            rows.append(spots[0] + (spots[1] - spots[0]) * i if any(inside) else None)
        return inner_pair(m, first + 2 * i, rows)

    def last_row(x):
        row = x - S
        step = 8
        columns = []

        def store(r, j, value, centre):
            f4[row, j - S] = value
            parts = [split_hi_lo(centre), split_hi_lo(value)]
            highs = [p[row, j - S, :NRHS, :] for p in pieces] + [p[0] for p in parts]
            lows = [p[row, j - S, NRHS:, :] for p in pieces] + [p[1] for p in parts]
            columns.append(jnp.concatenate(highs + lows, axis=0))

        for _ in mean_rows(f3, x, 1, range(S, S + by), store):
            if len(columns) == step:
                block = jnp.concatenate(columns, axis=1)
                acc[...] += lax.dot_general(
                    block, block[:ROWS], (((1,), (1,)), ((), ())), preferred_element_type=F32
                )
                columns.clear()
            yield

    def run(work):
        for _ in work:
            pass

    def weave(work, count, other, extra):
        done = 0
        for k, _ in enumerate(work):
            while done * count < extra * (k + 1):
                next(other, None)
                done += 1
        run(other)

    def rows_of(first, count, body):
        lax.fori_loop(first, first + count, body, 0, unroll=2)

    def pairs_of(m, *parts):
        def body(i, carry):
            x = S + m + 2 * i
            for columns in parts:
                run(inner_pair(m, x, (x - S, x + 1 - S), columns))
            return carry

        lax.fori_loop(0, bx // 2 - m, body, 0)

    def twice(work):
        def body(i, carry):
            work(i)
            return carry

        lax.fori_loop(0, 2, body, 0)

    def keep(m, first, count):
        src = f4.at[pl.ds(first, count)] if m == S else fields[m].at[pl.ds(S + first, count), pl.ds(S, by)]
        pltpu.make_async_copy(src, basis_hbm.at[m, pl.ds(first, count)], basis_sem).start()

    rows_of(S, bx, start_own)
    pl.semaphore_wait(barrier, len(peers))

    x_all, y_all = (0, bx), (0, by)
    x_top, x_low = (bx - S, S), (0, S)
    x_top3, x_low3 = (bx - S + 1, S - 1), (0, S - 1)
    y_top, y_low = (by - PAD, PAD), (0, PAD)
    routes = (
        ((right, gy), x_top, y_all, 0, PAD),
        ((left, gy), x_low, y_all, S + bx, PAD),
        ((gx, up), x_all, y_top, S, 0),
        ((gx, down), x_all, y_low, S, PAD + by),
        ((right, up), x_top3, y_top, 1, 0),
        ((right, down), x_top3, y_low, 1, PAD + by),
        ((left, up), x_low3, y_top, S + bx, 0),
        ((left, down), x_low3, y_low, S + bx, PAD + by),
    )
    face_copies = []
    for r, (peer, xs, ys, dx, dy) in enumerate(routes):
        copy = pltpu.make_async_remote_copy(
            src_ref=wide.at[:, pl.ds(S + xs[0], xs[1]), pl.ds(PAD + ys[0], ys[1])],
            dst_ref=wide.at[:, pl.ds(dx, xs[1]), pl.ds(dy, ys[1])],
            send_sem=face_send.at[r],
            recv_sem=face_recv.at[r],
            device_id=peer,
            device_id_type=MESH,
        )
        copy.start()
        face_copies.append(copy)
    keep(0, 0, bx)
    rows_of(S + 1, bx - 2, weight_inner)
    pairs_of(1, range(S + 1, S + by - 1))
    for copy in face_copies[2:4]:
        copy.wait_recv()
    rows_of(S, bx, mask_own)
    rows_of(S + 1, bx - 2, weight_sides)
    pairs_of(1, range(1, S + 1), range(S + by - 1, ey - 1))
    keep(1, 1, bx - 2)
    for m in range(2, S):
        pairs_of(m, None)
        keep(m, m, bx - 2 * m)

    for copy in face_copies[:2] + face_copies[4:]:
        copy.wait_recv()
    low, top, inner = S, bx, 2 * S
    wide_pair = 2 * ey
    twice(lambda i: weave(last_row(inner + i), by, start_far((2 * i, 2 * i + 1)), wide_pair))
    rows_of(1, S, weight_row)
    twice(lambda i: weave(last_row(inner + 2 + i), by, far_pair(1, 1, i), ey - 2))
    twice(lambda i: weave(last_row(inner + 4 + i), by, far_pair(2, 2, i), ey - 4))
    far = S + bx
    twice(lambda i: weave(last_row(inner + 6 + i), by, start_far((far + 2 * i, far + 2 * i + 1)), wide_pair))
    keep(S, S, bx - 2 * S)
    rows_of(far - 1, S, weight_row)
    twice(lambda i: run(far_pair(3, 3, i)))
    twice(lambda i: weave(last_row(low + i), by, far_pair(1, far - 1, i), ey - 2))
    twice(lambda i: weave(last_row(low + 2 + i), by, far_pair(2, far - 2, i), ey - 4))
    keep(S, 0, S)
    twice(lambda i: run(far_pair(3, far - 3, i)))
    for m in range(1, S):
        keep(m, 0, m)
        keep(m, bx - m, m)

    def last_top(x, carry):
        run(last_row(x))
        return carry

    lax.fori_loop(top, top + S, last_top, 0)
    keep(S, bx - S, S)

    both = acc[...]
    lane_g = lax.broadcasted_iota(jnp.int32, (ROWS, LANES), 1)
    cross = jnp.concatenate([both[ROWS:], jnp.zeros((ROWS, LANES - ROWS), F32)], axis=1)
    square = jnp.concatenate([cross, jnp.zeros((LANES - ROWS, LANES), F32)], axis=0)
    gram = jnp.concatenate([both[:ROWS], jnp.zeros((ROWS, LANES - ROWS), F32)], axis=1) + cross + square.T[:ROWS]
    lane_b = lane_g[:NRHS]
    blocks = [gram[m * NRHS : (m + 1) * NRHS] for m in range(S + 1)]
    part1[gy, :NRHS] = blocks[0] + jnp.where(lane_b < ROWS, 0.0, pltpu.roll(blocks[2], 48, 1))
    part1[gy, NRHS:] = jnp.where(
        lane_b < ROWS,
        blocks[1],
        jnp.where(lane_b < 112, pltpu.roll(blocks[3], 32, 1), pltpu.roll(blocks[4], 48, 1)),
    )

    sends = []

    def spread(k, peers_of, slots, slot):
        copies = []
        for peer in peers_of:
            copy = pltpu.make_async_remote_copy(
                src_ref=slots.at[slot],
                dst_ref=slots.at[slot],
                send_sem=ring_send.at[k],
                recv_sem=ring_recv.at[k],
                device_id=peer,
                device_id_type=MESH,
            )
            copy.start()
            copies.append(copy)
        others = slots.at[pl.ds(0, len(copies))]
        whole = pltpu.make_async_copy(others, others, ring_recv.at[k])
        whole.wait()
        sends.append(pltpu.make_async_copy(others, others, ring_send.at[k]))
        return jnp.sum(slots[...], axis=0)

    part2[xi] = spread(0, [at_y(o) for o in range(1, ny)], part1, gy)
    part3[zi] = spread(1, [at_x(o) for o in range(1, RING_X)], part2, xi)
    total_ref[...] = spread(2, [at_z(o) for o in range(1, ring_z)], part3, zi)

    for send in sends:
        send.wait()
    for copy in face_copies:
        copy.wait_send()
    pltpu.make_async_copy(basis_hbm, basis_hbm, basis_sem).wait()


def solve_table(total):
    top, low = total[:NRHS], total[NRHS:]
    blocks = [top, low, pltpu.roll(top, 80, 1), pltpu.roll(low, 96, 1), pltpu.roll(low, 80, 1)]
    upper = jnp.concatenate(blocks + [jnp.zeros((LANES - ROWS, LANES), F32)], axis=0)
    lane = lax.broadcasted_iota(jnp.int32, (LANES, LANES), 1)
    row = lax.broadcasted_iota(jnp.int32, (LANES, LANES), 0)
    keep = (lane // NRHS >= row // NRHS) & (lane < ROWS)
    upper = jnp.where(keep, upper, 0.0)
    gram = jnp.where(keep, upper, upper.T)
    down = gram[:BASIS] - gram[NRHS : BASIS + NRHS]
    lane64, row64 = lane[:BASIS], row[:BASIS]
    hess = down - pltpu.roll(down, LANES - NRHS, 1)
    work = jnp.where(lane64 < BASIS, hess, jnp.where(lane64 < ROWS, pltpu.roll(down, BASIS, 1), 0.0))
    for j in range(BASIS):
        pivot = work[j : j + 1, :]
        scaled = pivot / pivot[:, j : j + 1]
        column = work[:, j : j + 1]
        work = jnp.where(row64 == j, scaled, work - column * scaled)
    coeffs = jnp.where(lane64 < NRHS, pltpu.roll(work, LANES - BASIS, 1), 0.0)
    gap = jnp.zeros((NRHS, LANES), F32)
    full = jnp.concatenate([coeffs, gap], axis=0)
    moved = jnp.concatenate([gap, coeffs], axis=0)
    unit = jnp.where((lane[:ROWS] == row[:ROWS]) & (lane[:ROWS] < NRHS), 1.0, 0.0)
    pair = full + pltpu.roll(unit - (full - moved), NRHS, 1)
    tall = jnp.concatenate([pair, pair, jnp.zeros((2 * LANES - 2 * ROWS, LANES), F32)], axis=0)
    return jnp.concatenate([tall[:LANES].T, tall[LANES:].T], axis=1)[: 2 * NRHS]


def combine_kernel(basis_hbm, total_ref, sol_hbm, res_hbm, basis, sol, res, left_ref, basis_sem, sol_sem, res_sem):
    bx, by = basis_hbm.shape[1], basis_hbm.shape[2]
    group = bx // basis_sem.shape[0]
    pitch = sol.shape[2]

    def load(g):
        rows = pl.ds(g * group, group)
        return pltpu.make_async_copy(basis_hbm.at[:, rows], basis.at[:, rows], basis_sem.at[g])

    for g in range(bx // group):
        load(g).start()

    high, low = split_hi_lo(solve_table(total_ref[...]))
    left_ref[...] = jnp.concatenate([high, low], axis=0)
    left = left_ref[:, : 2 * ROWS]

    def combine_row(x):
        for y in range(0, by, 2):
            columns = []
            for k in range(2):
                parts = [split_hi_lo(basis[m, x, y + k]) for m in range(S + 1)]
                columns.append(jnp.concatenate([p[0] for p in parts] + [p[1] for p in parts], axis=0))
            both = jnp.dot(left, jnp.concatenate(columns, axis=1), preferred_element_type=F32)
            both = both[: 2 * NRHS] + both[2 * NRHS :]
            for k in range(2):
                part = both[:, k * LANES : (k + 1) * LANES]
                sol.at[x].reshape(NRHS * pitch, LANES)[pl.ds(y + k, NRHS, stride=pitch), :] = part[:NRHS]
                res.at[x].reshape(NRHS * pitch, LANES)[pl.ds(y + k, NRHS, stride=pitch), :] = part[NRHS:]
        pltpu.make_async_copy(sol.at[x, :, pl.ds(0, by)], sol_hbm.at[:, x], sol_sem).start()
        pltpu.make_async_copy(res.at[x, :, pl.ds(0, by)], res_hbm.at[:, x], res_sem).start()

    def body(g, carry):
        load(g).wait()
        for r in range(group):
            combine_row(g * group + r)
        return carry

    lax.fori_loop(0, bx // group, body, 0)
    pltpu.make_async_copy(sol_hbm, sol_hbm, sol_sem).wait()
    pltpu.make_async_copy(res_hbm, res_hbm, res_sem).wait()


def krylov_call(nx, ny, phase_label, tab_index, source_field, sigma_table, gain):
    bx, by = phase_label.shape[0], phase_label.shape[1]
    ex, ey = bx + 2 * S, by + 2 * S
    wide = (ex, by + 2 * PAD, LANES)
    ring_z = nx // RING_X
    hbm = pl.BlockSpec(memory_space=pl.ANY)
    vmem = pl.BlockSpec(memory_space=pltpu.VMEM)
    dma = pltpu.SemaphoreType.DMA
    packed = (2 * NRHS, LANES)
    return pl.pallas_call(
        functools.partial(krylov_kernel, nx, ny),
        out_shape=(
            jax.ShapeDtypeStruct((S + 1, bx, by, NRHS, LANES), F32),
            jax.ShapeDtypeStruct(packed, F32),
        ),
        in_specs=[hbm] * 5,
        out_specs=(hbm, vmem),
        scratch_shapes=[
            pltpu.SMEM(sigma_table.shape, F32),
            pltpu.VMEM(gain.shape, F32),
            pltpu.VMEM((bx, by, LANES), jnp.int32),
            pltpu.VMEM(wide, jnp.int32),
            pltpu.VMEM((3,) + wide, F32),
            pltpu.VMEM(wide, F32),
            pltpu.VMEM(wide, F32),
            pltpu.VMEM((6,) + wide, F32),
        ]
        + [pltpu.VMEM((ex, ey, NRHS, LANES), F32)] * S
        + [
            pltpu.VMEM((bx, by, NRHS, LANES), F32),
            pltpu.VMEM((bx + 1, by, 2 * NRHS, LANES), BF16),
            pltpu.VMEM((bx + 1, by, 2 * NRHS, LANES), BF16),
            pltpu.VMEM((bx + 1, by, 2 * NRHS, LANES), BF16),
            pltpu.VMEM((2 * ROWS, ROWS), F32),
            pltpu.VMEM((ny,) + packed, F32),
            pltpu.VMEM((RING_X,) + packed, F32),
            pltpu.VMEM((ring_z,) + packed, F32),
            dma((5,)),
            dma((8,)),
            dma((8,)),
            dma(()),
            dma((3,)),
            dma((3,)),
        ],
        compiler_params=pltpu.CompilerParams(
            collective_id=0, has_side_effects=True, vmem_limit_bytes=60 * 2**20
        ),
    )(phase_label, tab_index, source_field, sigma_table, gain)


def combine_call(basis, total):
    bx, by = basis.shape[1], basis.shape[2]
    hbm = pl.BlockSpec(memory_space=pl.ANY)
    vmem = pl.BlockSpec(memory_space=pltpu.VMEM)
    dma = pltpu.SemaphoreType.DMA
    out = jax.ShapeDtypeStruct((NRHS, bx, by, LANES), F32)
    return pl.pallas_call(
        combine_kernel,
        out_shape=(out, out),
        in_specs=[hbm, vmem],
        out_specs=(hbm, hbm),
        scratch_shapes=[
            pltpu.VMEM(basis.shape, F32),
            pltpu.VMEM((bx, NRHS, by + PAD, LANES), F32),
            pltpu.VMEM((bx, NRHS, by + PAD, LANES), F32),
            pltpu.VMEM((4 * NRHS, 2 * LANES), BF16),
            dma((bx // 2,)),
            dma(()),
            dma(()),
        ],
        compiler_params=pltpu.CompilerParams(vmem_limit_bytes=56 * 2**20),
    )(basis, total)


def solution(mesh):
    nx, ny = mesh.shape["gx"], mesh.shape["gy"]

    def shards(phase_label, tab_index, source_field, sigma_table, pattern_gain):
        basis, total = krylov_call(nx, ny, phase_label, tab_index, source_field, sigma_table, pattern_gain)
        return combine_call(basis, total)

    return jax.shard_map(
        shards,
        mesh=mesh,
        in_specs=(P("gx", "gy", None), P("gx", "gy", None), P("gx", "gy", None), P(), P()),
        out_specs=(P(None, "gx", "gy", None), P(None, "gx", "gy", None)),
        check_vma=False,
    )
```

```python
import functools

import jax
import jax.numpy as jnp
from jax import lax
from jax.experimental import pallas as pl
from jax.experimental.pallas import tpu as pltpu
from jax.sharding import PartitionSpec as P

S = 4
NRHS = 16
LANES = 128
PAD = 8
RING_X = 4
MESH = pl.DeviceIdType.MESH
F32 = jnp.float32
BF16 = jnp.bfloat16
ROWS = (S + 1) * NRHS
BASIS = S * NRHS


def split_hi_lo(value):
    high = value.astype(BF16)
    low = (value - high.astype(F32)).astype(BF16)
    return high, low


def lane_pick(table, index):
    numbers = lax.GatherDimensionNumbers(
        offset_dims=(),
        collapsed_slice_dims=(1,),
        start_index_map=(1,),
        operand_batching_dims=(0,),
        start_indices_batching_dims=(0,),
    )
    return lax.gather(
        table, index[..., None], numbers, (1, 1), mode=lax.GatherScatterMode.PROMISE_IN_BOUNDS
    )


def krylov_kernel(nx, ny, phase_hbm, tab_hbm, source_hbm, sigma_hbm, gain_hbm, basis_hbm, total_ref,
                  sigma_ref, gain_ref, phase_own, tab_ext, wide, conduct, charge, weight, f0, f1, f2, f3, f4, p0, p1, p2, acc,
                  part1, part2, part3, own_sem, face_send, face_recv, basis_sem, ring_send, ring_recv):
    bx, by = phase_hbm.shape[0], phase_hbm.shape[1]
    ex = bx + 2 * S
    ey = by + 2 * S
    gx, gy = lax.axis_index("gx"), lax.axis_index("gy")
    xi, zi = lax.rem(gx, RING_X), lax.div(gx, RING_X)
    ring_z = nx // RING_X
    right, left = lax.rem(gx + 1, nx), lax.rem(gx + nx - 1, nx)
    up, down = lax.rem(gy + 1, ny), lax.rem(gy + ny - 1, ny)

    def at_y(o):
        return gx, lax.rem(gy + o, ny)

    def at_x(o):
        return zi * RING_X + lax.rem(xi + o, RING_X), gy

    def at_z(o):
        return lax.rem(zi + o, ring_z) * RING_X + xi, gy

    own = (pl.ds(S, bx), pl.ds(PAD, by))
    own_copies = [
        pltpu.make_async_copy(phase_hbm, phase_own, own_sem.at[0]),
        pltpu.make_async_copy(tab_hbm, tab_ext.at[own], own_sem.at[1]),
        pltpu.make_async_copy(source_hbm, wide.at[(2,) + own], own_sem.at[2]),
        pltpu.make_async_copy(sigma_hbm, sigma_ref, own_sem.at[3]),
        pltpu.make_async_copy(gain_hbm, gain_ref, own_sem.at[4]),
    ]
    for copy in own_copies:
        copy.start()
    faces = ((right, gy), (left, gy), (right, up), (right, down), (left, up), (left, down))
    peers = faces + tuple(at_y(o) for o in range(1, ny)) + tuple(at_x(o) for o in range(1, RING_X)) + tuple(
        at_z(o) for o in range(1, ring_z))
    barrier = pltpu.get_barrier_semaphore()
    for peer in peers:
        pl.semaphore_signal(barrier, inc=1, device_id=peer, device_id_type=MESH)
    corner = jnp.zeros((PAD, LANES), F32)
    for a in range(3):
        for x in (0, ex - 1):
            for y in (0, PAD + by):
                wide[a, x, y : y + PAD, :] = corner
    acc[...] = jnp.zeros_like(acc)
    for copy in own_copies:
        copy.wait()
    sigma0, sigma1, sigma2 = sigma_ref[0], sigma_ref[1], sigma_ref[2]
    gain = jnp.concatenate([gain_ref[...], jnp.zeros((NRHS, LANES - gain_ref.shape[1]), F32)], axis=1)

    def fill_row(r, carry):
        phase = phase_own[r]
        value = jnp.where(phase == 0, sigma0, jnp.where(phase == 1, sigma1, sigma2))
        wide[0, r + S, PAD : PAD + by, :] = value
        conduct[r + S, PAD : PAD + by, :] = value
        wide[1, r + S, PAD : PAD + by, :] = tab_ext[r + S, PAD : PAD + by, :].astype(F32)
        return carry

    lax.fori_loop(0, bx, fill_row, 0, unroll=4)
    lane = lax.broadcasted_iota(jnp.int32, (PAD * 2 + by, LANES), 1)
    row_y = lax.broadcasted_iota(jnp.int32, (PAD * 2 + by, LANES), 0) + (gy * by - PAD)
    in_y = (row_y >= 0) & (row_y < ny * by)

    fields = (f0, f1, f2, f3)
    pieces = (p0, p1, p2)

    def keep_pieces(m, row, column, value):
        high, low = split_hi_lo(value)
        pieces[m][row, column, :NRHS, :] = high
        pieces[m][row, column, NRHS:, :] = low

    def start_columns(x, columns, strength, row=None):
        for j in columns:
            tab = jnp.broadcast_to(tab_ext[x, pl.ds(j + PAD - S, 1), :], (NRHS, LANES))
            value = lane_pick(gain, tab) * jnp.broadcast_to(strength(j + PAD - S), (NRHS, LANES))
            f0[x, j] = value
            if row is not None:
                keep_pieces(0, row, j - S, value)
            yield

    tabs = gain_ref.shape[1]
    rest = gain_ref[...]
    gain_parts = []
    for _ in range(3):
        gain_parts.append(rest.astype(BF16))
        rest = rest - gain_parts[-1].astype(F32)
    gain_stack = jnp.concatenate(gain_parts, axis=0)
    tab_row = lax.broadcasted_iota(jnp.int32, (tabs, LANES), 0)

    def start_pairs(x, columns, strength, row=None):
        for k in range(0, len(columns), 2):
            pair = columns[k : k + 2]
            picks = []
            for j in pair:
                tab = jnp.broadcast_to(tab_ext[x, pl.ds(j + PAD - S, 1), :], (tabs, LANES))
                picks.append(jnp.where(tab == tab_row, 1.0, 0.0).astype(BF16))
            parts = jnp.dot(gain_stack, jnp.concatenate(picks, axis=1), preferred_element_type=F32)
            picked = parts[:NRHS] + (parts[NRHS : 2 * NRHS] + parts[2 * NRHS :])
            for n, j in enumerate(pair):
                value = picked[:, n * LANES : (n + 1) * LANES]
                value = value * jnp.broadcast_to(strength(j + PAD - S), (NRHS, LANES))
                f0[x, j] = value
                if row is not None:
                    keep_pieces(0, row, j - S, value)
            yield

    def start_own(x, carry):
        def strength(y):
            return wide[2, x, pl.ds(y, 1), :]

        split = S + 16
        weave(
            start_columns(x, range(S, split), strength, x - S),
            16,
            start_pairs(x, range(split, S + by), strength, x - S),
            (by - 16) // 2,
        )
        return carry

    def mask_row(x, sides):
        row_x = gx * bx + x - S
        in_x = (row_x >= 0) & (row_x < nx * bx)
        for first, count in sides:
            at = slice(first, first + count)
            inside = in_y[at] & in_x
            conduct[x, at, :] = jnp.where(inside, wide[0, x, at, :], 0.0)
            charge[x, at, :] = jnp.where(inside, wide[2, x, at, :], 0.0)
            tab_ext[x, at, :] = wide[1, x, at, :].astype(jnp.int32)

    def mask_own(x, carry):
        mask_row(x, ((0, PAD), (PAD + by, PAD)))

        def strength(y):
            return charge[x, pl.ds(y, 1), :]

        weave(
            start_columns(x, range(S), strength), S, start_pairs(x, range(S + by, ey), strength), S // 2
        )
        return carry

    def start_far(rows):
        for x in rows:
            mask_row(x, ((0, 2 * PAD + by),))
        for x in rows:
            yield from start_columns(x, range(ey), lambda y, x=x: charge[x, pl.ds(y, 1), :])

    def weight_part(x, first, count, start, stop):
        at = slice(first, first + count)
        c = conduct[x, at, :]
        zero = jnp.zeros_like(c)
        xm = c + conduct[x - 1, at, :]
        xp = c + conduct[x + 1, at, :]
        ym = c + pltpu.roll(c, 1, 0)
        yp = c + pltpu.roll(c, count - 1, 0)
        low, top = lane[at] > 0, lane[at] < LANES - 1
        zm = c + jnp.where(low, pltpu.roll(c, 1, 1), zero)
        zp = c + jnp.where(top, pltpu.roll(c, LANES - 1, 1), zero)
        total = ((xm + xp) + (ym + yp)) + (zm + zp)
        inside = c > 0
        inverse = jnp.where(inside, 1.0 / jnp.where(inside, total, 1.0), 0.0)
        parts = (xm, xp, ym, yp, jnp.where(low, zm, zero), jnp.where(top, zp, zero))
        for d, part in enumerate(parts):
            weight[d, x, start:stop, :] = (part * inverse)[start - first : stop - first]

    def weight_row(x, carry):
        weight_part(x, 0, by + 2 * PAD, 0, by + 2 * PAD)
        return carry

    def weight_inner(x, carry):
        weight_part(x, PAD, by, PAD, PAD + by)
        return carry

    def weight_sides(x, carry):
        weight_part(x, 0, 2 * PAD, 0, PAD + 1)
        weight_part(x, by, 2 * PAD, PAD + by - 1, by + 2 * PAD)
        return carry

    def mean_rows(src, x, count, columns, store):
        before = [src[x + r, columns[0] - 1] for r in range(count)]
        centre = [src[x + r, columns[0]] for r in range(count)]
        for j in columns:
            after = [src[x + r, j + 1] for r in range(count)]
            edge = [src[x - 1, j]] + centre + [src[x + count, j]]
            for r in range(count):
                w = [jnp.broadcast_to(weight[d, x + r, pl.ds(j + PAD - S, 1), :], (NRHS, LANES)) for d in range(6)]
                value = (w[0] * edge[r] + w[1] * edge[r + 2]) + (w[2] * before[r] + w[3] * after[r])
                value = value + (w[4] * pltpu.roll(centre[r], 1, 1) + w[5] * pltpu.roll(centre[r], LANES - 1, 1))
                store(r, j, value, centre[r])
            before, centre = centre, after
            yield

    def inner_pair(m, x, rows, columns=None):
        def store(r, j, value, centre):
            fields[m][x + r, j] = value
            if m < S - 1 and rows[r] is not None and S <= j < S + by:
                keep_pieces(m, rows[r], j - S, value)

        return mean_rows(fields[m - 1], x, 2, range(m, ey - m) if columns is None else columns, store)

    def far_pair(m, first, i):
        rows = []
        for r in range(2):
            spots = [first + 2 * k + r - S for k in range(2)]
            inside = [0 <= spot < bx for spot in spots]
            spots = [spot if ok else bx for spot, ok in zip(spots, inside)]
            rows.append(spots[0] + (spots[1] - spots[0]) * i if any(inside) else None)
        return inner_pair(m, first + 2 * i, rows)

    def last_row(x):
        row = x - S
        step = 8
        columns = []

        def store(r, j, value, centre):
            f4[row, j - S] = value
            parts = [split_hi_lo(centre), split_hi_lo(value)]
            highs = [p[row, j - S, :NRHS, :] for p in pieces] + [p[0] for p in parts]
            lows = [p[row, j - S, NRHS:, :] for p in pieces] + [p[1] for p in parts]
            columns.append(jnp.concatenate(highs + lows, axis=0))

        for _ in mean_rows(f3, x, 1, range(S, S + by), store):
            if len(columns) == step:
                block = jnp.concatenate(columns, axis=1)
                acc[...] += lax.dot_general(
                    block, block[:ROWS], (((1,), (1,)), ((), ())), preferred_element_type=F32
                )
                columns.clear()
            yield

    def run(work):
        for _ in work:
            pass

    def weave(work, count, other, extra):
        done = 0
        for k, _ in enumerate(work):
            while done * count < extra * (k + 1):
                next(other, None)
                done += 1
        run(other)

    def rows_of(first, count, body, unroll=2):
        lax.fori_loop(first, first + count, body, 0, unroll=unroll)

    def pairs_of(m, *parts, unroll=1):
        def body(i, carry):
            x = S + m + 2 * i
            for columns in parts:
                run(inner_pair(m, x, (x - S, x + 1 - S), columns))
            return carry

        lax.fori_loop(0, bx // 2 - m, body, 0, unroll=unroll)

    def twice(work):
        def body(i, carry):
            work(i)
            return carry

        lax.fori_loop(0, 2, body, 0)

    def keep(m, first, count):
        src = f4.at[pl.ds(first, count)] if m == S else fields[m].at[pl.ds(S + first, count), pl.ds(S, by)]
        pltpu.make_async_copy(src, basis_hbm.at[m, pl.ds(first, count)], basis_sem).start()

    rows_of(S, bx, start_own, 4)
    pl.semaphore_wait(barrier, len(peers))

    x_all, y_all = (0, bx), (0, by)
    x_top, x_low = (bx - S, S), (0, S)
    x_top3, x_low3 = (bx - S + 1, S - 1), (0, S - 1)
    y_top, y_low = (by - PAD, PAD), (0, PAD)
    routes = (
        ((right, gy), x_top, y_all, 0, PAD),
        ((left, gy), x_low, y_all, S + bx, PAD),
        ((gx, up), x_all, y_top, S, 0),
        ((gx, down), x_all, y_low, S, PAD + by),
        ((right, up), x_top3, y_top, 1, 0),
        ((right, down), x_top3, y_low, 1, PAD + by),
        ((left, up), x_low3, y_top, S + bx, 0),
        ((left, down), x_low3, y_low, S + bx, PAD + by),
    )
    face_copies = []
    for r, (peer, xs, ys, dx, dy) in enumerate(routes):
        copy = pltpu.make_async_remote_copy(
            src_ref=wide.at[:, pl.ds(S + xs[0], xs[1]), pl.ds(PAD + ys[0], ys[1])],
            dst_ref=wide.at[:, pl.ds(dx, xs[1]), pl.ds(dy, ys[1])],
            send_sem=face_send.at[r],
            recv_sem=face_recv.at[r],
            device_id=peer,
            device_id_type=MESH,
        )
        copy.start()
        face_copies.append(copy)
    keep(0, 0, bx)
    rows_of(S + 1, bx - 2, weight_inner, 7)
    pairs_of(1, range(S + 1, S + by - 1))
    for copy in face_copies[2:4]:
        copy.wait_recv()
    rows_of(S, bx, mask_own, 4)
    rows_of(S + 1, bx - 2, weight_sides, 7)
    pairs_of(1, range(1, S + 1), range(S + by - 1, ey - 1), unroll=7)
    keep(1, 1, bx - 2)
    for m in range(2, S):
        pairs_of(m, None, unroll=3 if m == 2 else 1)
        keep(m, m, bx - 2 * m)

    for copy in face_copies[:2] + face_copies[4:]:
        copy.wait_recv()
    low, top, inner = S, bx, 2 * S
    wide_pair = 2 * ey
    twice(lambda i: weave(last_row(inner + i), by, start_far((2 * i, 2 * i + 1)), wide_pair))
    rows_of(1, S, weight_row, S)
    twice(lambda i: weave(last_row(inner + 2 + i), by, far_pair(1, 1, i), ey - 2))
    twice(lambda i: weave(last_row(inner + 4 + i), by, far_pair(2, 2, i), ey - 4))
    far = S + bx
    twice(lambda i: weave(last_row(inner + 6 + i), by, start_far((far + 2 * i, far + 2 * i + 1)), wide_pair))
    keep(S, S, bx - 2 * S)
    rows_of(far - 1, S, weight_row, S)
    twice(lambda i: run(far_pair(3, 3, i)))
    twice(lambda i: weave(last_row(low + i), by, far_pair(1, far - 1, i), ey - 2))
    twice(lambda i: weave(last_row(low + 2 + i), by, far_pair(2, far - 2, i), ey - 4))
    keep(S, 0, S)
    twice(lambda i: run(far_pair(3, far - 3, i)))
    for m in range(1, S):
        keep(m, 0, m)
        keep(m, bx - m, m)

    def last_top(x, carry):
        run(last_row(x))
        return carry

    lax.fori_loop(top, top + S, last_top, 0)
    keep(S, bx - S, S)

    both = acc[...]
    lane_g = lax.broadcasted_iota(jnp.int32, (ROWS, LANES), 1)
    cross = jnp.concatenate([both[ROWS:], jnp.zeros((ROWS, LANES - ROWS), F32)], axis=1)
    square = jnp.concatenate([cross, jnp.zeros((LANES - ROWS, LANES), F32)], axis=0)
    gram = jnp.concatenate([both[:ROWS], jnp.zeros((ROWS, LANES - ROWS), F32)], axis=1) + cross + square.T[:ROWS]
    lane_b = lane_g[:NRHS]
    blocks = [gram[m * NRHS : (m + 1) * NRHS] for m in range(S + 1)]
    part1[gy, :NRHS] = blocks[0] + jnp.where(lane_b < ROWS, 0.0, pltpu.roll(blocks[2], 48, 1))
    part1[gy, NRHS:] = jnp.where(
        lane_b < ROWS,
        blocks[1],
        jnp.where(lane_b < 112, pltpu.roll(blocks[3], 32, 1), pltpu.roll(blocks[4], 48, 1)),
    )

    sends = []

    def spread(k, peers_of, slots, slot):
        copies = []
        for peer in peers_of:
            copy = pltpu.make_async_remote_copy(
                src_ref=slots.at[slot],
                dst_ref=slots.at[slot],
                send_sem=ring_send.at[k],
                recv_sem=ring_recv.at[k],
                device_id=peer,
                device_id_type=MESH,
            )
            copy.start()
            copies.append(copy)
        others = slots.at[pl.ds(0, len(copies))]
        whole = pltpu.make_async_copy(others, others, ring_recv.at[k])
        whole.wait()
        sends.append(pltpu.make_async_copy(others, others, ring_send.at[k]))
        return jnp.sum(slots[...], axis=0)

    part2[xi] = spread(0, [at_y(o) for o in range(1, ny)], part1, gy)
    part3[zi] = spread(1, [at_x(o) for o in range(1, RING_X)], part2, xi)
    total_ref[...] = spread(2, [at_z(o) for o in range(1, ring_z)], part3, zi)

    for send in sends:
        send.wait()
    for copy in face_copies:
        copy.wait_send()
    pltpu.make_async_copy(basis_hbm, basis_hbm, basis_sem).wait()


def solve_table(total):
    top, low = total[:NRHS], total[NRHS:]
    blocks = [top, low, pltpu.roll(top, 80, 1), pltpu.roll(low, 96, 1), pltpu.roll(low, 80, 1)]
    upper = jnp.concatenate(blocks + [jnp.zeros((LANES - ROWS, LANES), F32)], axis=0)
    lane = lax.broadcasted_iota(jnp.int32, (LANES, LANES), 1)
    row = lax.broadcasted_iota(jnp.int32, (LANES, LANES), 0)
    keep = (lane // NRHS >= row // NRHS) & (lane < ROWS)
    upper = jnp.where(keep, upper, 0.0)
    gram = jnp.where(keep, upper, upper.T)
    down = gram[:BASIS] - gram[NRHS : BASIS + NRHS]
    lane64, row64 = lane[:BASIS], row[:BASIS]
    hess = down - pltpu.roll(down, LANES - NRHS, 1)
    work = jnp.where(lane64 < BASIS, hess, jnp.where(lane64 < ROWS, pltpu.roll(down, BASIS, 1), 0.0))
    for j in range(BASIS):
        pivot = work[j : j + 1, :]
        scaled = pivot / pivot[:, j : j + 1]
        column = work[:, j : j + 1]
        work = jnp.where(row64 == j, scaled, work - column * scaled)
    coeffs = jnp.where(lane64 < NRHS, pltpu.roll(work, LANES - BASIS, 1), 0.0)
    gap = jnp.zeros((NRHS, LANES), F32)
    full = jnp.concatenate([coeffs, gap], axis=0)
    moved = jnp.concatenate([gap, coeffs], axis=0)
    unit = jnp.where((lane[:ROWS] == row[:ROWS]) & (lane[:ROWS] < NRHS), 1.0, 0.0)
    pair = full + pltpu.roll(unit - (full - moved), NRHS, 1)
    tall = jnp.concatenate([pair, pair, jnp.zeros((2 * LANES - 2 * ROWS, LANES), F32)], axis=0)
    return jnp.concatenate([tall[:LANES].T, tall[LANES:].T], axis=1)[: 2 * NRHS]


def combine_kernel(basis_hbm, total_ref, sol_hbm, res_hbm, basis, sol, res, left_ref, basis_sem, sol_sem, res_sem):
    bx, by = basis_hbm.shape[1], basis_hbm.shape[2]
    group = bx // basis_sem.shape[0]
    pitch = sol.shape[2]

    def load(g):
        rows = pl.ds(g * group, group)
        return pltpu.make_async_copy(basis_hbm.at[:, rows], basis.at[:, rows], basis_sem.at[g])

    for g in range(bx // group):
        load(g).start()

    high, low = split_hi_lo(solve_table(total_ref[...]))
    left_ref[...] = jnp.concatenate([high, low], axis=0)
    left = left_ref[:, : 2 * ROWS]

    def combine_row(x):
        for y in range(0, by, 2):
            columns = []
            for k in range(2):
                parts = [split_hi_lo(basis[m, x, y + k]) for m in range(S + 1)]
                columns.append(jnp.concatenate([p[0] for p in parts] + [p[1] for p in parts], axis=0))
            both = jnp.dot(left, jnp.concatenate(columns, axis=1), preferred_element_type=F32)
            both = both[: 2 * NRHS] + both[2 * NRHS :]
            for k in range(2):
                part = both[:, k * LANES : (k + 1) * LANES]
                sol.at[x].reshape(NRHS * pitch, LANES)[pl.ds(y + k, NRHS, stride=pitch), :] = part[:NRHS]
                res.at[x].reshape(NRHS * pitch, LANES)[pl.ds(y + k, NRHS, stride=pitch), :] = part[NRHS:]
        pltpu.make_async_copy(sol.at[x, :, pl.ds(0, by)], sol_hbm.at[:, x], sol_sem).start()
        pltpu.make_async_copy(res.at[x, :, pl.ds(0, by)], res_hbm.at[:, x], res_sem).start()

    def body(g, carry):
        load(g).wait()
        for r in range(group):
            combine_row(g * group + r)
        return carry

    lax.fori_loop(0, bx // group, body, 0)
    pltpu.make_async_copy(sol_hbm, sol_hbm, sol_sem).wait()
    pltpu.make_async_copy(res_hbm, res_hbm, res_sem).wait()


def krylov_call(nx, ny, phase_label, tab_index, source_field, sigma_table, gain):
    bx, by = phase_label.shape[0], phase_label.shape[1]
    ex, ey = bx + 2 * S, by + 2 * S
    wide = (ex, by + 2 * PAD, LANES)
    ring_z = nx // RING_X
    hbm = pl.BlockSpec(memory_space=pl.ANY)
    vmem = pl.BlockSpec(memory_space=pltpu.VMEM)
    dma = pltpu.SemaphoreType.DMA
    packed = (2 * NRHS, LANES)
    return pl.pallas_call(
        functools.partial(krylov_kernel, nx, ny),
        out_shape=(
            jax.ShapeDtypeStruct((S + 1, bx, by, NRHS, LANES), F32),
            jax.ShapeDtypeStruct(packed, F32),
        ),
        in_specs=[hbm] * 5,
        out_specs=(hbm, vmem),
        scratch_shapes=[
            pltpu.SMEM(sigma_table.shape, F32),
            pltpu.VMEM(gain.shape, F32),
            pltpu.VMEM((bx, by, LANES), jnp.int32),
            pltpu.VMEM(wide, jnp.int32),
            pltpu.VMEM((3,) + wide, F32),
            pltpu.VMEM(wide, F32),
            pltpu.VMEM(wide, F32),
            pltpu.VMEM((6,) + wide, F32),
        ]
        + [pltpu.VMEM((ex, ey, NRHS, LANES), F32)] * S
        + [
            pltpu.VMEM((bx, by, NRHS, LANES), F32),
            pltpu.VMEM((bx + 1, by, 2 * NRHS, LANES), BF16),
            pltpu.VMEM((bx + 1, by, 2 * NRHS, LANES), BF16),
            pltpu.VMEM((bx + 1, by, 2 * NRHS, LANES), BF16),
            pltpu.VMEM((2 * ROWS, ROWS), F32),
            pltpu.VMEM((ny,) + packed, F32),
            pltpu.VMEM((RING_X,) + packed, F32),
            pltpu.VMEM((ring_z,) + packed, F32),
            dma((5,)),
            dma((8,)),
            dma((8,)),
            dma(()),
            dma((3,)),
            dma((3,)),
        ],
        compiler_params=pltpu.CompilerParams(
            collective_id=0, has_side_effects=True, vmem_limit_bytes=60 * 2**20
        ),
    )(phase_label, tab_index, source_field, sigma_table, gain)


def combine_call(basis, total):
    bx, by = basis.shape[1], basis.shape[2]
    hbm = pl.BlockSpec(memory_space=pl.ANY)
    vmem = pl.BlockSpec(memory_space=pltpu.VMEM)
    dma = pltpu.SemaphoreType.DMA
    out = jax.ShapeDtypeStruct((NRHS, bx, by, LANES), F32)
    return pl.pallas_call(
        combine_kernel,
        out_shape=(out, out),
        in_specs=[hbm, vmem],
        out_specs=(hbm, hbm),
        scratch_shapes=[
            pltpu.VMEM(basis.shape, F32),
            pltpu.VMEM((bx, NRHS, by + PAD, LANES), F32),
            pltpu.VMEM((bx, NRHS, by + PAD, LANES), F32),
            pltpu.VMEM((4 * NRHS, 2 * LANES), BF16),
            dma((bx // 4,)),
            dma(()),
            dma(()),
        ],
        compiler_params=pltpu.CompilerParams(vmem_limit_bytes=56 * 2**20),
    )(basis, total)


def solution(mesh):
    nx, ny = mesh.shape["gx"], mesh.shape["gy"]

    def shards(phase_label, tab_index, source_field, sigma_table, pattern_gain):
        basis, total = krylov_call(nx, ny, phase_label, tab_index, source_field, sigma_table, pattern_gain)
        return combine_call(basis, total)

    return jax.shard_map(
        shards,
        mesh=mesh,
        in_specs=(P("gx", "gy", None), P("gx", "gy", None), P("gx", "gy", None), P(), P()),
        out_specs=(P(None, "gx", "gy", None), P(None, "gx", "gy", None)),
        check_vma=False,
    )
```

```python
import functools

import jax
import jax.numpy as jnp
from jax import lax
from jax.experimental import pallas as pl
from jax.experimental.pallas import tpu as pltpu
from jax.sharding import PartitionSpec as P

S = 4
NRHS = 16
LANES = 128
PAD = 8
RING_X = 4
MESH = pl.DeviceIdType.MESH
F32 = jnp.float32
BF16 = jnp.bfloat16
ROWS = (S + 1) * NRHS
BASIS = S * NRHS


def split_hi_lo(value):
    high = value.astype(BF16)
    low = (value - high.astype(F32)).astype(BF16)
    return high, low


def lane_pick(table, index):
    numbers = lax.GatherDimensionNumbers(
        offset_dims=(),
        collapsed_slice_dims=(1,),
        start_index_map=(1,),
        operand_batching_dims=(0,),
        start_indices_batching_dims=(0,),
    )
    return lax.gather(
        table, index[..., None], numbers, (1, 1), mode=lax.GatherScatterMode.PROMISE_IN_BOUNDS
    )


def krylov_kernel(nx, ny, phase_hbm, tab_hbm, source_hbm, sigma_hbm, gain_hbm, basis_hbm, total_ref,
                  sigma_ref, gain_ref, phase_own, tab_ext, wide, conduct, charge, weight, f0, f1, f2, f3, f4, p0, p1, p2, acc,
                  part1, part2, part3, own_sem, face_send, face_recv, basis_sem, ring_send, ring_recv):
    bx, by = phase_hbm.shape[0], phase_hbm.shape[1]
    ex = bx + 2 * S
    ey = by + 2 * S
    gx, gy = lax.axis_index("gx"), lax.axis_index("gy")
    xi, zi = lax.rem(gx, RING_X), lax.div(gx, RING_X)
    ring_z = nx // RING_X
    right, left = lax.rem(gx + 1, nx), lax.rem(gx + nx - 1, nx)
    up, down = lax.rem(gy + 1, ny), lax.rem(gy + ny - 1, ny)

    def at_y(o):
        return gx, lax.rem(gy + o, ny)

    def at_x(o):
        return zi * RING_X + lax.rem(xi + o, RING_X), gy

    def at_z(o):
        return lax.rem(zi + o, ring_z) * RING_X + xi, gy

    own = (pl.ds(S, bx), pl.ds(PAD, by))
    own_copies = [
        pltpu.make_async_copy(phase_hbm, phase_own, own_sem.at[0]),
        pltpu.make_async_copy(tab_hbm, tab_ext.at[own], own_sem.at[1]),
        pltpu.make_async_copy(source_hbm, wide.at[(2,) + own], own_sem.at[2]),
        pltpu.make_async_copy(sigma_hbm, sigma_ref, own_sem.at[3]),
        pltpu.make_async_copy(gain_hbm, gain_ref, own_sem.at[4]),
    ]
    for copy in own_copies:
        copy.start()
    faces = ((right, gy), (left, gy), (right, up), (right, down), (left, up), (left, down))
    peers = faces + tuple(at_y(o) for o in range(1, ny)) + tuple(at_x(o) for o in range(1, RING_X)) + tuple(
        at_z(o) for o in range(1, ring_z))
    barrier = pltpu.get_barrier_semaphore()
    for peer in peers:
        pl.semaphore_signal(barrier, inc=1, device_id=peer, device_id_type=MESH)
    corner = jnp.zeros((PAD, LANES), F32)
    for a in range(3):
        for x in (0, ex - 1):
            for y in (0, PAD + by):
                wide[a, x, y : y + PAD, :] = corner
    acc[...] = jnp.zeros_like(acc)
    for copy in own_copies:
        copy.wait()
    sigma0, sigma1, sigma2 = sigma_ref[0], sigma_ref[1], sigma_ref[2]
    gain = jnp.concatenate([gain_ref[...], jnp.zeros((NRHS, LANES - gain_ref.shape[1]), F32)], axis=1)

    def fill_row(r, carry):
        phase = phase_own[r]
        value = jnp.where(phase == 0, sigma0, jnp.where(phase == 1, sigma1, sigma2))
        wide[0, r + S, PAD : PAD + by, :] = value
        conduct[r + S, PAD : PAD + by, :] = value
        wide[1, r + S, PAD : PAD + by, :] = tab_ext[r + S, PAD : PAD + by, :].astype(F32)
        return carry

    lax.fori_loop(0, bx, fill_row, 0, unroll=4)
    lane = lax.broadcasted_iota(jnp.int32, (PAD * 2 + by, LANES), 1)
    row_y = lax.broadcasted_iota(jnp.int32, (PAD * 2 + by, LANES), 0) + (gy * by - PAD)
    in_y = (row_y >= 0) & (row_y < ny * by)

    fields = (f0, f1, f2, f3)
    pieces = (p0, p1, p2)

    def keep_pieces(m, row, column, value):
        high, low = split_hi_lo(value)
        pieces[m][row, column, :NRHS, :] = high
        pieces[m][row, column, NRHS:, :] = low

    def start_columns(x, columns, strength, row=None):
        for j in columns:
            tab = jnp.broadcast_to(tab_ext[x, pl.ds(j + PAD - S, 1), :], (NRHS, LANES))
            value = lane_pick(gain, tab) * jnp.broadcast_to(strength(j + PAD - S), (NRHS, LANES))
            f0[x, j] = value
            if row is not None:
                keep_pieces(0, row, j - S, value)
            yield

    tabs = gain_ref.shape[1]
    rest = gain_ref[...]
    gain_parts = []
    for _ in range(3):
        gain_parts.append(rest.astype(BF16))
        rest = rest - gain_parts[-1].astype(F32)
    gain_stack = jnp.concatenate(gain_parts, axis=0)
    tab_row = lax.broadcasted_iota(jnp.int32, (tabs, LANES), 0)

    def start_pairs(x, columns, strength, row=None):
        for k in range(0, len(columns), 2):
            pair = columns[k : k + 2]
            picks = []
            for j in pair:
                tab = jnp.broadcast_to(tab_ext[x, pl.ds(j + PAD - S, 1), :], (tabs, LANES))
                picks.append(jnp.where(tab == tab_row, 1.0, 0.0).astype(BF16))
            parts = jnp.dot(gain_stack, jnp.concatenate(picks, axis=1), preferred_element_type=F32)
            picked = parts[:NRHS] + (parts[NRHS : 2 * NRHS] + parts[2 * NRHS :])
            for n, j in enumerate(pair):
                value = picked[:, n * LANES : (n + 1) * LANES]
                value = value * jnp.broadcast_to(strength(j + PAD - S), (NRHS, LANES))
                f0[x, j] = value
                if row is not None:
                    keep_pieces(0, row, j - S, value)
            yield

    def start_own(x, carry):
        def strength(y):
            return wide[2, x, pl.ds(y, 1), :]

        split = S + 16
        weave(
            start_columns(x, range(S, split), strength, x - S),
            16,
            start_pairs(x, range(split, S + by), strength, x - S),
            (by - 16) // 2,
        )
        return carry

    def mask_row(x, sides):
        row_x = gx * bx + x - S
        in_x = (row_x >= 0) & (row_x < nx * bx)
        for first, count in sides:
            at = slice(first, first + count)
            inside = in_y[at] & in_x
            conduct[x, at, :] = jnp.where(inside, wide[0, x, at, :], 0.0)
            charge[x, at, :] = jnp.where(inside, wide[2, x, at, :], 0.0)
            tab_ext[x, at, :] = wide[1, x, at, :].astype(jnp.int32)

    def mask_own(x, carry):
        mask_row(x, ((0, PAD), (PAD + by, PAD)))

        def strength(y):
            return charge[x, pl.ds(y, 1), :]

        weave(
            start_columns(x, range(S), strength), S, start_pairs(x, range(S + by, ey), strength), S // 2
        )
        return carry

    def start_far(rows):
        for x in rows:
            mask_row(x, ((0, 2 * PAD + by),))
        for x in rows:
            yield from start_columns(x, range(ey), lambda y, x=x: charge[x, pl.ds(y, 1), :])

    def weight_part(x, first, count, start, stop):
        at = slice(first, first + count)
        c = conduct[x, at, :]
        zero = jnp.zeros_like(c)
        xm = c + conduct[x - 1, at, :]
        xp = c + conduct[x + 1, at, :]
        ym = c + pltpu.roll(c, 1, 0)
        yp = c + pltpu.roll(c, count - 1, 0)
        low, top = lane[at] > 0, lane[at] < LANES - 1
        zm = c + jnp.where(low, pltpu.roll(c, 1, 1), zero)
        zp = c + jnp.where(top, pltpu.roll(c, LANES - 1, 1), zero)
        total = ((xm + xp) + (ym + yp)) + (zm + zp)
        inside = c > 0
        inverse = jnp.where(inside, 1.0 / jnp.where(inside, total, 1.0), 0.0)
        parts = (xm, xp, ym, yp, jnp.where(low, zm, zero), jnp.where(top, zp, zero))
        for d, part in enumerate(parts):
            weight[d, x, start:stop, :] = (part * inverse)[start - first : stop - first]

    def weight_row(x, carry):
        weight_part(x, 0, by + 2 * PAD, 0, by + 2 * PAD)
        return carry

    def weight_inner(x, carry):
        weight_part(x, PAD, by, PAD, PAD + by)
        return carry

    def weight_sides(x, carry):
        weight_part(x, 0, 2 * PAD, 0, PAD + 1)
        weight_part(x, by, 2 * PAD, PAD + by - 1, by + 2 * PAD)
        return carry

    def mean_rows(src, x, count, columns, store):
        before = [src[x + r, columns[0] - 1] for r in range(count)]
        centre = [src[x + r, columns[0]] for r in range(count)]
        for j in columns:
            after = [src[x + r, j + 1] for r in range(count)]
            edge = [src[x - 1, j]] + centre + [src[x + count, j]]
            for r in range(count):
                w = [jnp.broadcast_to(weight[d, x + r, pl.ds(j + PAD - S, 1), :], (NRHS, LANES)) for d in range(6)]
                value = (w[0] * edge[r] + w[1] * edge[r + 2]) + (w[2] * before[r] + w[3] * after[r])
                value = value + (w[4] * pltpu.roll(centre[r], 1, 1) + w[5] * pltpu.roll(centre[r], LANES - 1, 1))
                store(r, j, value, centre[r])
            before, centre = centre, after
            yield

    def inner_pair(m, x, rows, columns=None):
        def store(r, j, value, centre):
            fields[m][x + r, j] = value
            if m < S - 1 and rows[r] is not None and S <= j < S + by:
                keep_pieces(m, rows[r], j - S, value)

        return mean_rows(fields[m - 1], x, 2, range(m, ey - m) if columns is None else columns, store)

    def far_pair(m, first, i):
        rows = []
        for r in range(2):
            spots = [first + 2 * k + r - S for k in range(2)]
            inside = [0 <= spot < bx for spot in spots]
            spots = [spot if ok else bx for spot, ok in zip(spots, inside)]
            rows.append(spots[0] + (spots[1] - spots[0]) * i if any(inside) else None)
        return inner_pair(m, first + 2 * i, rows)

    def last_row(x):
        row = x - S
        step = 8
        columns = []

        def store(r, j, value, centre):
            f4[row, j - S] = value
            parts = [split_hi_lo(centre), split_hi_lo(value)]
            highs = [p[row, j - S, :NRHS, :] for p in pieces] + [p[0] for p in parts]
            lows = [p[row, j - S, NRHS:, :] for p in pieces] + [p[1] for p in parts]
            columns.append(jnp.concatenate(highs + lows, axis=0))

        for _ in mean_rows(f3, x, 1, range(S, S + by), store):
            if len(columns) == step:
                block = jnp.concatenate(columns, axis=1)
                acc[...] += lax.dot_general(
                    block, block[:ROWS], (((1,), (1,)), ((), ())), preferred_element_type=F32
                )
                columns.clear()
            yield

    def run(work):
        for _ in work:
            pass

    def weave(work, count, other, extra):
        done = 0
        for k, _ in enumerate(work):
            while done * count < extra * (k + 1):
                next(other, None)
                done += 1
        run(other)

    def rows_of(first, count, body, unroll=2):
        lax.fori_loop(first, first + count, body, 0, unroll=unroll)

    def pairs_of(m, *parts, unroll=1):
        def body(i, carry):
            x = S + m + 2 * i
            for columns in parts:
                run(inner_pair(m, x, (x - S, x + 1 - S), columns))
            return carry

        lax.fori_loop(0, bx // 2 - m, body, 0, unroll=unroll)

    def twice(work, unroll=1):
        def body(i, carry):
            work(i)
            return carry

        lax.fori_loop(0, 2, body, 0, unroll=unroll)

    def keep(m, first, count):
        src = f4.at[pl.ds(first, count)] if m == S else fields[m].at[pl.ds(S + first, count), pl.ds(S, by)]
        pltpu.make_async_copy(src, basis_hbm.at[m, pl.ds(first, count)], basis_sem).start()

    rows_of(S, bx, start_own, 4)
    pl.semaphore_wait(barrier, len(peers))

    x_all, y_all = (0, bx), (0, by)
    x_top, x_low = (bx - S, S), (0, S)
    x_top3, x_low3 = (bx - S + 1, S - 1), (0, S - 1)
    y_top, y_low = (by - PAD, PAD), (0, PAD)
    routes = (
        ((right, gy), x_top, y_all, 0, PAD),
        ((left, gy), x_low, y_all, S + bx, PAD),
        ((gx, up), x_all, y_top, S, 0),
        ((gx, down), x_all, y_low, S, PAD + by),
        ((right, up), x_top3, y_top, 1, 0),
        ((right, down), x_top3, y_low, 1, PAD + by),
        ((left, up), x_low3, y_top, S + bx, 0),
        ((left, down), x_low3, y_low, S + bx, PAD + by),
    )
    face_copies = []
    for r, (peer, xs, ys, dx, dy) in enumerate(routes):
        copy = pltpu.make_async_remote_copy(
            src_ref=wide.at[:, pl.ds(S + xs[0], xs[1]), pl.ds(PAD + ys[0], ys[1])],
            dst_ref=wide.at[:, pl.ds(dx, xs[1]), pl.ds(dy, ys[1])],
            send_sem=face_send.at[r],
            recv_sem=face_recv.at[r],
            device_id=peer,
            device_id_type=MESH,
        )
        copy.start()
        face_copies.append(copy)
    keep(0, 0, bx)
    rows_of(S + 1, bx - 2, weight_inner, 7)
    pairs_of(1, range(S + 1, S + by - 1))
    for copy in face_copies[2:4]:
        copy.wait_recv()
    rows_of(S, bx, mask_own, 4)
    rows_of(S + 1, bx - 2, weight_sides, 7)
    pairs_of(1, range(1, S + 1), range(S + by - 1, ey - 1), unroll=7)
    keep(1, 1, bx - 2)
    for m in range(2, S):
        pairs_of(m, None, unroll=3 if m == 2 else 5)
        keep(m, m, bx - 2 * m)

    for copy in face_copies[:2] + face_copies[4:]:
        copy.wait_recv()
    low, top, inner = S, bx, 2 * S
    wide_pair = 2 * ey
    twice(lambda i: weave(last_row(inner + i), by, start_far((2 * i, 2 * i + 1)), wide_pair))
    rows_of(1, S, weight_row, S)
    twice(lambda i: weave(last_row(inner + 2 + i), by, far_pair(1, 1, i), ey - 2))
    twice(lambda i: weave(last_row(inner + 4 + i), by, far_pair(2, 2, i), ey - 4))
    far = S + bx
    twice(lambda i: weave(last_row(inner + 6 + i), by, start_far((far + 2 * i, far + 2 * i + 1)), wide_pair))
    keep(S, S, bx - 2 * S)
    rows_of(far - 1, S, weight_row, S)
    twice(lambda i: run(far_pair(3, 3, i)), 2)
    twice(lambda i: weave(last_row(low + i), by, far_pair(1, far - 1, i), ey - 2))
    twice(lambda i: weave(last_row(low + 2 + i), by, far_pair(2, far - 2, i), ey - 4))
    keep(S, 0, S)
    twice(lambda i: run(far_pair(3, far - 3, i)), 2)
    for m in range(1, S):
        keep(m, 0, m)
        keep(m, bx - m, m)

    def last_top(x, carry):
        run(last_row(x))
        return carry

    lax.fori_loop(top, top + S, last_top, 0, unroll=2)
    keep(S, bx - S, S)

    both = acc[...]
    lane_g = lax.broadcasted_iota(jnp.int32, (ROWS, LANES), 1)
    cross = jnp.concatenate([both[ROWS:], jnp.zeros((ROWS, LANES - ROWS), F32)], axis=1)
    square = jnp.concatenate([cross, jnp.zeros((LANES - ROWS, LANES), F32)], axis=0)
    gram = jnp.concatenate([both[:ROWS], jnp.zeros((ROWS, LANES - ROWS), F32)], axis=1) + cross + square.T[:ROWS]
    lane_b = lane_g[:NRHS]
    blocks = [gram[m * NRHS : (m + 1) * NRHS] for m in range(S + 1)]
    part1[gy, :NRHS] = blocks[0] + jnp.where(lane_b < ROWS, 0.0, pltpu.roll(blocks[2], 48, 1))
    part1[gy, NRHS:] = jnp.where(
        lane_b < ROWS,
        blocks[1],
        jnp.where(lane_b < 112, pltpu.roll(blocks[3], 32, 1), pltpu.roll(blocks[4], 48, 1)),
    )

    sends = []

    def spread(k, peers_of, slots, slot):
        copies = []
        for peer in peers_of:
            copy = pltpu.make_async_remote_copy(
                src_ref=slots.at[slot],
                dst_ref=slots.at[slot],
                send_sem=ring_send.at[k],
                recv_sem=ring_recv.at[k],
                device_id=peer,
                device_id_type=MESH,
            )
            copy.start()
            copies.append(copy)
        others = slots.at[pl.ds(0, len(copies))]
        whole = pltpu.make_async_copy(others, others, ring_recv.at[k])
        whole.wait()
        sends.append(pltpu.make_async_copy(others, others, ring_send.at[k]))
        return jnp.sum(slots[...], axis=0)

    part2[xi] = spread(0, [at_y(o) for o in range(1, ny)], part1, gy)
    part3[zi] = spread(1, [at_x(o) for o in range(1, RING_X)], part2, xi)
    total_ref[...] = spread(2, [at_z(o) for o in range(1, ring_z)], part3, zi)

    for send in sends:
        send.wait()
    for copy in face_copies:
        copy.wait_send()
    pltpu.make_async_copy(basis_hbm, basis_hbm, basis_sem).wait()


def solve_table(total):
    top, low = total[:NRHS], total[NRHS:]
    blocks = [top, low, pltpu.roll(top, 80, 1), pltpu.roll(low, 96, 1), pltpu.roll(low, 80, 1)]
    upper = jnp.concatenate(blocks + [jnp.zeros((LANES - ROWS, LANES), F32)], axis=0)
    lane = lax.broadcasted_iota(jnp.int32, (LANES, LANES), 1)
    row = lax.broadcasted_iota(jnp.int32, (LANES, LANES), 0)
    keep = (lane // NRHS >= row // NRHS) & (lane < ROWS)
    upper = jnp.where(keep, upper, 0.0)
    gram = jnp.where(keep, upper, upper.T)
    down = gram[:BASIS] - gram[NRHS : BASIS + NRHS]
    lane64, row64 = lane[:BASIS], row[:BASIS]
    hess = down - pltpu.roll(down, LANES - NRHS, 1)
    work = jnp.where(lane64 < BASIS, hess, jnp.where(lane64 < ROWS, pltpu.roll(down, BASIS, 1), 0.0))
    for j in range(BASIS):
        pivot = work[j : j + 1, :]
        scaled = pivot / pivot[:, j : j + 1]
        column = work[:, j : j + 1]
        work = jnp.where(row64 == j, scaled, work - column * scaled)
    coeffs = jnp.where(lane64 < NRHS, pltpu.roll(work, LANES - BASIS, 1), 0.0)
    gap = jnp.zeros((NRHS, LANES), F32)
    full = jnp.concatenate([coeffs, gap], axis=0)
    moved = jnp.concatenate([gap, coeffs], axis=0)
    unit = jnp.where((lane[:ROWS] == row[:ROWS]) & (lane[:ROWS] < NRHS), 1.0, 0.0)
    pair = full + pltpu.roll(unit - (full - moved), NRHS, 1)
    tall = jnp.concatenate([pair, pair, jnp.zeros((2 * LANES - 2 * ROWS, LANES), F32)], axis=0)
    return jnp.concatenate([tall[:LANES].T, tall[LANES:].T], axis=1)[: 2 * NRHS]


def combine_kernel(basis_hbm, total_ref, sol_hbm, res_hbm, basis, sol, res, left_ref, basis_sem, sol_sem, res_sem):
    bx, by = basis_hbm.shape[1], basis_hbm.shape[2]
    group = bx // basis_sem.shape[0]
    pitch = sol.shape[2]

    def load(g):
        rows = pl.ds(g * group, group)
        return pltpu.make_async_copy(basis_hbm.at[:, rows], basis.at[:, rows], basis_sem.at[g])

    for g in range(bx // group):
        load(g).start()

    high, low = split_hi_lo(solve_table(total_ref[...]))
    left_ref[...] = jnp.concatenate([high, low], axis=0)
    left = left_ref[:, : 2 * ROWS]

    def combine_row(x):
        for y in range(0, by, 2):
            columns = []
            for k in range(2):
                parts = [split_hi_lo(basis[m, x, y + k]) for m in range(S + 1)]
                columns.append(jnp.concatenate([p[0] for p in parts] + [p[1] for p in parts], axis=0))
            both = jnp.dot(left, jnp.concatenate(columns, axis=1), preferred_element_type=F32)
            both = both[: 2 * NRHS] + both[2 * NRHS :]
            for k in range(2):
                part = both[:, k * LANES : (k + 1) * LANES]
                sol.at[x].reshape(NRHS * pitch, LANES)[pl.ds(y + k, NRHS, stride=pitch), :] = part[:NRHS]
                res.at[x].reshape(NRHS * pitch, LANES)[pl.ds(y + k, NRHS, stride=pitch), :] = part[NRHS:]
        pltpu.make_async_copy(sol.at[x, :, pl.ds(0, by)], sol_hbm.at[:, x], sol_sem).start()
        pltpu.make_async_copy(res.at[x, :, pl.ds(0, by)], res_hbm.at[:, x], res_sem).start()

    def body(g, carry):
        load(g).wait()
        for r in range(group):
            combine_row(g * group + r)
        return carry

    lax.fori_loop(0, bx // group, body, 0)
    pltpu.make_async_copy(sol_hbm, sol_hbm, sol_sem).wait()
    pltpu.make_async_copy(res_hbm, res_hbm, res_sem).wait()


def krylov_call(nx, ny, phase_label, tab_index, source_field, sigma_table, gain):
    bx, by = phase_label.shape[0], phase_label.shape[1]
    ex, ey = bx + 2 * S, by + 2 * S
    wide = (ex, by + 2 * PAD, LANES)
    ring_z = nx // RING_X
    hbm = pl.BlockSpec(memory_space=pl.ANY)
    vmem = pl.BlockSpec(memory_space=pltpu.VMEM)
    dma = pltpu.SemaphoreType.DMA
    packed = (2 * NRHS, LANES)
    return pl.pallas_call(
        functools.partial(krylov_kernel, nx, ny),
        out_shape=(
            jax.ShapeDtypeStruct((S + 1, bx, by, NRHS, LANES), F32),
            jax.ShapeDtypeStruct(packed, F32),
        ),
        in_specs=[hbm] * 5,
        out_specs=(hbm, vmem),
        scratch_shapes=[
            pltpu.SMEM(sigma_table.shape, F32),
            pltpu.VMEM(gain.shape, F32),
            pltpu.VMEM((bx, by, LANES), jnp.int32),
            pltpu.VMEM(wide, jnp.int32),
            pltpu.VMEM((3,) + wide, F32),
            pltpu.VMEM(wide, F32),
            pltpu.VMEM(wide, F32),
            pltpu.VMEM((6,) + wide, F32),
        ]
        + [pltpu.VMEM((ex, ey, NRHS, LANES), F32)] * S
        + [
            pltpu.VMEM((bx, by, NRHS, LANES), F32),
            pltpu.VMEM((bx + 1, by, 2 * NRHS, LANES), BF16),
            pltpu.VMEM((bx + 1, by, 2 * NRHS, LANES), BF16),
            pltpu.VMEM((bx + 1, by, 2 * NRHS, LANES), BF16),
            pltpu.VMEM((2 * ROWS, ROWS), F32),
            pltpu.VMEM((ny,) + packed, F32),
            pltpu.VMEM((RING_X,) + packed, F32),
            pltpu.VMEM((ring_z,) + packed, F32),
            dma((5,)),
            dma((8,)),
            dma((8,)),
            dma(()),
            dma((3,)),
            dma((3,)),
        ],
        compiler_params=pltpu.CompilerParams(
            collective_id=0, has_side_effects=True, vmem_limit_bytes=60 * 2**20
        ),
    )(phase_label, tab_index, source_field, sigma_table, gain)


def combine_call(basis, total):
    bx, by = basis.shape[1], basis.shape[2]
    hbm = pl.BlockSpec(memory_space=pl.ANY)
    vmem = pl.BlockSpec(memory_space=pltpu.VMEM)
    dma = pltpu.SemaphoreType.DMA
    out = jax.ShapeDtypeStruct((NRHS, bx, by, LANES), F32)
    return pl.pallas_call(
        combine_kernel,
        out_shape=(out, out),
        in_specs=[hbm, vmem],
        out_specs=(hbm, hbm),
        scratch_shapes=[
            pltpu.VMEM(basis.shape, F32),
            pltpu.VMEM((bx, NRHS, by + PAD, LANES), F32),
            pltpu.VMEM((bx, NRHS, by + PAD, LANES), F32),
            pltpu.VMEM((4 * NRHS, 2 * LANES), BF16),
            dma((bx // 4,)),
            dma(()),
            dma(()),
        ],
        compiler_params=pltpu.CompilerParams(vmem_limit_bytes=56 * 2**20),
    )(basis, total)


def solution(mesh):
    nx, ny = mesh.shape["gx"], mesh.shape["gy"]

    def shards(phase_label, tab_index, source_field, sigma_table, pattern_gain):
        basis, total = krylov_call(nx, ny, phase_label, tab_index, source_field, sigma_table, pattern_gain)
        return combine_call(basis, total)

    return jax.shard_map(
        shards,
        mesh=mesh,
        in_specs=(P("gx", "gy", None), P("gx", "gy", None), P("gx", "gy", None), P(), P()),
        out_specs=(P(None, "gx", "gy", None), P(None, "gx", "gy", None)),
        check_vma=False,
    )
```
